32 devices in a mesh: dp: 4 (over x, core), ctx: 8 (over z, y).
Axes of the slice: x: 2, y: 2, z: 4, core: 2. Of those that a mesh axis runs over, the one named last changes fastest.
Arguments:
- queries: bfloat16 [4, 2048, 512], P('dp', 'ctx'), may hold values from -40 to 40
- key_rows: bfloat16 [4, 2048, 512], P('dp', 'ctx'), may hold values from -40 to 40
- value_rows: bfloat16 [4, 2048, 512], P('dp', 'ctx'), may hold values from -24 to 24
- out_weight: bfloat16 [512, 1024], P('dp'), may hold values from -0.5 to 0.5
- head_weight: bfloat16 [1024, 1024], P('dp'), may hold values from -1.1953125 to 1.1953125
- conv_weight: float32 [9, 1024], replicated, may hold values from -3 to 3
- lengths: int32 [4], P('dp'), may hold values from 1 to 2048, 2730 in all
- label_mask: int32 [4, 2048], P('dp', 'ctx'), may hold values 0 or 1
- targets: int32 [4, 2048], P('dp', 'ctx'), may hold values from 0 to 1023
Outputs:
- loss: float32 [], replicated
- d_queries: bfloat16 [4, 2048, 512], P('dp', 'ctx')
- d_keys: bfloat16 [4, 2048, 512], P('dp', 'ctx')
- d_values: bfloat16 [4, 2048, 512], P('dp', 'ctx')
- d_conv: float32 [9, 1024], replicated
The draws below stay inside these ranges and needn't reach their ends.
Inputs may be any that keep to these rules, and one draw needn't show every extreme that they name: `lengths`: the longest recording has exactly 2048 frames.
All inputs are finite; a program needn't handle non-finite values. No bound on the sum of `lengths` or of `label_mask` on one device may be relied on, other than what follows from the above.
Results may differ from the reference program's by a relative error of at most 0.034.
Values may be sent and summed in bfloat16 or wider, within the bound.
No kernel may reach another device: no remote copies, remote signals or barrier semaphores. Data moves between devices by JAX's collectives and lax.ppermute only.
A program may use at most 64 MiB of HBM per device.

```python
import math
import jax
import jax.numpy as jnp
import numpy as np
from jax import lax

D = 1024
HEAD_DIM = 128
WINDOW = 128
TAPS = 9
VOCAB = 1024
TOK_DEV = 256
ATT_W = 512
SEQ = 2048
RECS = 4


def drawn_pair(key):
    shape = (RECS, SEQ, ATT_W)
    query_rows = jnp.clip(jax.random.normal(jax.random.fold_in(key, 101), shape, jnp.float32), -4.0, 4.0)
    key_vectors = jnp.clip(jax.random.normal(jax.random.fold_in(key, 202), shape, jnp.float32), -4.0, 4.0)
    return (query_rows, key_vectors)


def draw_queries(key, part):
    return drawn_pair(key)[0].astype(jnp.bfloat16)


def draw_key_rows(key, part):
    return drawn_pair(key)[1].astype(jnp.bfloat16)


def with_ends(entries, key, least, top_value):
    spot = [jax.random.randint(jax.random.fold_in(key, axis), (), 0, length) for axis, length in enumerate(entries.shape)]
    main_axis = entries.shape.index(max(entries.shape))
    neighbour = spot[:main_axis] + [(spot[main_axis] + 1) % entries.shape[main_axis]] + spot[main_axis + 1:]
    return entries.at[tuple(spot)].set(least).at[tuple(neighbour)].set(top_value)


def block_levels(key, dims, shards, low, high):
    level, own = 1.0, jax.random.fold_in(key, 6)
    for axis_at, shards_of in shards:
        draws = jnp.exp(jax.random.uniform(jax.random.fold_in(own, axis_at), (shards_of,), jnp.float32, low / len(shards), high / len(shards)))
        level = level * jnp.repeat(draws, dims[axis_at] // shards_of).reshape([-1 if axis == axis_at else 1 for axis in range(len(dims))])
    return level


def cumulative_ranks(amount, slope):
    weights = [(1 << 20) // math.isqrt(grade ** slope) + 1 for grade in range(1, amount + 1)]
    scale = 1 + sum(weights) // (1 << 30)
    return np.cumsum(np.array([max(1, weight // scale) for weight in weights]))


def ranked(stream_key, extent, amount, lean):
    grid = cumulative_ranks(amount, lean)
    ticket = jax.random.randint(jax.random.fold_in(stream_key, 1), extent, 0, int(grid[amount - 1]))
    grade = jnp.searchsorted(jnp.asarray(grid, jnp.int32), ticket, side="right")
    return jax.random.permutation(jax.random.fold_in(stream_key, 2), amount)[grade].astype(jnp.int32)


def profile(amount, total, reach, lean):
    loads = [(1 << 20) // math.isqrt(standing ** lean) + 1 for standing in range(2, amount + 1)]
    surplus, holding = total - reach - (amount - 1), [1] * (amount - 1)
    while surplus > 0:
        candidates = [i for i in range(amount - 1) if holding[i] < reach]
        pool, remaining = sum([loads[i] for i in candidates]), surplus
        for i in candidates:
            more = min(reach - holding[i], max(1, remaining * loads[i] // pool), surplus)
            holding[i] = holding[i] + more
            surplus = surplus - more
    return np.array([reach] + holding)


def ragged(key, amount, total, most, skew):
    if amount == 2:
        one = jax.random.randint(key, (), max(1, total - most), min(most, total - 1) + 1)
        return jnp.stack([one, total - one])
    tallies = jnp.asarray(profile(amount, total, most, skew), jnp.int32)
    twos = (amount - 1) // 2
    donor, receiver = tallies[1:1 + 2 * twos:2], tallies[2:2 + 2 * twos:2]
    room = jnp.minimum(donor - 1, most - receiver)
    moved = jax.random.randint(jax.random.fold_in(key, 1), (twos,), 0, 1 << 20) % (room + 1)
    tallies = tallies.at[1:1 + 2 * twos:2].set(donor - moved).at[2:2 + 2 * twos:2].set(receiver + moved)
    return tallies[jax.random.permutation(jax.random.fold_in(key, 2), amount)]


def gaussian(stream_key, shape, deviation, reach, split=(), kind=jnp.bfloat16):
    values = deviation * jax.random.normal(stream_key, shape, jnp.float32)
    if split:
        values = values * block_levels(stream_key, shape, split, -0.22, 0.18)
    return jnp.clip(values, -reach, reach).astype(kind)


def setup_inputs(seed: int = 0) -> dict:
    streams_of = jax.random.split(jax.random.key(seed), 10)
    queries = draw_queries(jax.random.fold_in(streams_of[9], 71), 0)
    key_rows = draw_key_rows(jax.random.fold_in(streams_of[9], 71), 0)
    value_rows = gaussian(streams_of[2], (RECS, SEQ, ATT_W), 4.0, 24.0, ((0, 4), (1, 8)))
    out_weight = gaussian(streams_of[3], (ATT_W, D), (ATT_W // 4) ** -0.5, 0.5, ((0, 4),))
    head_weight = gaussian(streams_of[4], (D, VOCAB), 0.2, 1.1953125, ((0, 4),))
    conv_weight = gaussian(streams_of[5], (TAPS, D), 0.5, 3.0, (), jnp.float32)
    lengths = ragged(streams_of[6], RECS, SEQ * RECS // 3, SEQ, 2).astype(jnp.int32)
    label_mask = with_ends((jax.random.randint(streams_of[7], (RECS, SEQ), 0, 4) < 3).astype(jnp.int32), jax.random.fold_in(streams_of[7], 1), 0, 1)
    targets = with_ends(ranked(streams_of[8], (RECS, SEQ), VOCAB, 2), jax.random.fold_in(streams_of[8], 3), 0, VOCAB - 1).astype(jnp.int32)
    return {"queries": queries, "key_rows": key_rows, "value_rows": value_rows, "out_weight": out_weight, "head_weight": head_weight, "conv_weight": conv_weight, "lengths": lengths, "label_mask": label_mask, "targets": targets}


def band_scores(query_heads, key_heads, query_pos, key_pos, length, factor):
    product = jnp.einsum('qhd,khd->hqk', query_heads, key_heads) * factor
    inside = (jnp.abs(query_pos[:, None] - key_pos[None, :]) <= WINDOW) & (key_pos[None, :] >= 0) & (key_pos[None, :] < length)
    return jnp.where(inside[None], product, -1e+30)

def one_recording(queries, key_rows, value_rows, length, label_mask, targets, out_weight, head_weight, conv_weight):
    head_count = ATT_W // HEAD_DIM
    factor = 1.0 / math.sqrt(HEAD_DIM)
    margin = (TAPS - 1) // 2
    blocks = SEQ // TOK_DEV
    ext_len = TOK_DEV + 2 * WINDOW
    key_pad = jnp.pad(key_rows, ((WINDOW, WINDOW), (0, 0)))
    value_pad = jnp.pad(value_rows, ((WINDOW, WINDOW), (0, 0)))

    def pieces(block):
        offset = (block * TOK_DEV).astype(jnp.int32)
        query_heads = lax.dynamic_slice_in_dim(queries, offset, TOK_DEV, 0).astype(jnp.float32).reshape(TOK_DEV, head_count, HEAD_DIM)
        key_heads = lax.dynamic_slice_in_dim(key_pad, offset, ext_len, 0).astype(jnp.float32).reshape(ext_len, head_count, HEAD_DIM)
        value_heads = lax.dynamic_slice_in_dim(value_pad, offset, ext_len, 0).astype(jnp.float32).reshape(ext_len, head_count, HEAD_DIM)
        query_pos = offset + jnp.arange(TOK_DEV, dtype=jnp.int32)
        key_pos = offset - WINDOW + jnp.arange(ext_len, dtype=jnp.int32)
        scores = band_scores(query_heads, key_heads, query_pos, key_pos, length, factor)
        return (offset, query_heads, key_heads, value_heads, scores)

    def forward_block(block):
        offset, query_heads, key_heads, value_heads, scores = pieces(block)
        row_max = lax.optimization_barrier(jnp.max(scores, axis=-1))
        log_total = row_max + jnp.log(lax.optimization_barrier(jnp.sum(jnp.exp(scores - row_max[..., None]), axis=-1)))
        prob_half = jnp.exp(scores - log_total[..., None]).astype(jnp.bfloat16)
        attn = jnp.einsum('hqk,khd->qhd', prob_half.astype(jnp.float32), value_heads).astype(jnp.bfloat16)
        return (attn.reshape(TOK_DEV, ATT_W), log_total)
    block_ids = jnp.arange(blocks, dtype=jnp.int32)
    attn_blocks, totals = lax.map(forward_block, block_ids)
    attn = attn_blocks.reshape(SEQ, ATT_W)
    position = jnp.arange(SEQ, dtype=jnp.int32)
    live = position < length
    hidden = jnp.dot(attn, out_weight, preferred_element_type=jnp.float32)
    hidden = jnp.where(live[:, None], hidden, 0.0)
    hidden_pad = jnp.pad(hidden, ((margin, margin), (0, 0)))
    conv = jnp.zeros((SEQ, D), jnp.float32)
    for tap in range(TAPS):
        conv = conv + conv_weight[tap] * hidden_pad[tap:tap + SEQ]
    sigma = jax.nn.sigmoid(conv)
    gated = (conv * sigma).astype(jnp.bfloat16)
    logits = jnp.dot(gated, head_weight, preferred_element_type=jnp.float32)
    top = lax.optimization_barrier(jnp.max(logits, axis=-1, keepdims=True))
    log_norm = top[:, 0] + jnp.log(lax.optimization_barrier(jnp.sum(jnp.exp(logits - top), axis=-1)))
    target_hit = targets[:, None] == jnp.arange(VOCAB, dtype=jnp.int32)[None, :]
    picked = lax.optimization_barrier(jnp.sum(jnp.where(target_hit, logits, 0.0), axis=-1))
    selected = ((label_mask == 1) & live).astype(jnp.float32)
    loss_sum = jnp.sum(selected * (log_norm - picked))
    count = jnp.sum(selected)
    soft = jnp.exp(logits - log_norm[:, None])
    dlogits = (selected[:, None] * (soft - target_hit.astype(jnp.float32))).astype(jnp.bfloat16)
    d_gated = jnp.dot(dlogits, head_weight.T, preferred_element_type=jnp.float32)
    d_pre = d_gated * sigma * (1.0 + conv * (1.0 - sigma))
    conv_grad = jnp.stack([lax.optimization_barrier(jnp.sum(d_pre * hidden_pad[tap:tap + SEQ], axis=0)) for tap in range(TAPS)])
    d_pad = jnp.pad(d_pre, ((margin, margin), (0, 0)))
    d_hidden = jnp.zeros((SEQ, D), jnp.float32)
    for tap in range(TAPS):
        d_hidden = d_hidden + conv_weight[tap] * d_pad[2 * margin - tap:2 * margin - tap + SEQ]
    d_hidden = jnp.where(live[:, None], d_hidden, 0.0).astype(jnp.bfloat16)
    d_attn = jnp.dot(d_hidden, out_weight.T, preferred_element_type=jnp.float32).astype(jnp.bfloat16)

    def backward_block(carry, block):
        key_acc, value_acc = carry
        offset, query_heads, key_heads, value_heads, scores = pieces(block)
        log_total = totals[block]
        probs = jnp.exp(scores - log_total[..., None])
        prob_half = probs.astype(jnp.bfloat16)
        d_heads = lax.dynamic_slice_in_dim(d_attn, offset, TOK_DEV, 0).astype(jnp.float32).reshape(TOK_DEV, head_count, HEAD_DIM)
        a_heads = lax.dynamic_slice_in_dim(attn, offset, TOK_DEV, 0).astype(jnp.float32).reshape(TOK_DEV, head_count, HEAD_DIM)
        row_delta = lax.optimization_barrier(jnp.sum(d_heads * a_heads, axis=-1)).T
        d_probs = jnp.einsum('qhd,khd->hqk', d_heads, value_heads)
        d_scores = (probs * (d_probs - row_delta[..., None])).astype(jnp.bfloat16).astype(jnp.float32)
        d_query = (jnp.einsum('hqk,khd->qhd', d_scores, key_heads) * factor).astype(jnp.bfloat16)
        key_part = (jnp.einsum('hqk,qhd->khd', d_scores, query_heads) * factor).reshape(ext_len, ATT_W)
        value_part = jnp.einsum('hqk,qhd->khd', prob_half.astype(jnp.float32), d_heads).reshape(ext_len, ATT_W)
        key_acc = lax.dynamic_update_slice_in_dim(key_acc, lax.dynamic_slice_in_dim(key_acc, offset, ext_len, 0) + key_part, offset, 0)
        value_acc = lax.dynamic_update_slice_in_dim(value_acc, lax.dynamic_slice_in_dim(value_acc, offset, ext_len, 0) + value_part, offset, 0)
        return ((key_acc, value_acc), d_query.reshape(TOK_DEV, ATT_W))
    zeros = jnp.zeros((SEQ + 2 * WINDOW, ATT_W), jnp.float32)
    (key_acc, value_acc), d_query_blocks = lax.scan(backward_block, (zeros, zeros), block_ids)
    d_queries = d_query_blocks.reshape(SEQ, ATT_W)
    d_keys = key_acc[WINDOW:WINDOW + SEQ].astype(jnp.bfloat16)
    d_values = value_acc[WINDOW:WINDOW + SEQ].astype(jnp.bfloat16)
    return (d_queries, d_keys, d_values, loss_sum, count, conv_grad)

def reference(queries, key_rows, value_rows, out_weight, head_weight, conv_weight, lengths, label_mask, targets):

    def single(items):
        return one_recording(items[0], items[1], items[2], items[3], items[4], items[5], out_weight, head_weight, conv_weight)
    d_queries, d_keys, d_values, loss_sums, counts, conv_grads = lax.map(single, (queries, key_rows, value_rows, lengths, label_mask, targets))
    count = jnp.sum(counts)
    loss = jnp.sum(loss_sums) / count
    d_conv = lax.optimization_barrier(jnp.sum(conv_grads, axis=0)) / jnp.sqrt(count)
    return (loss, d_queries, d_keys, d_values, d_conv)
```

```python
import functools
import math

import jax
import jax.numpy as jnp
from jax import lax
from jax.experimental import pallas as pl
from jax.experimental.pallas import tpu as pltpu
from jax.sharding import PartitionSpec as P

HEAD_DIM = 128
WINDOW = 128
TAPS = 9
MARGIN = (TAPS - 1) // 2
EDGE = 8
HALO = WINDOW + 2 * EDGE
LOW = -1e30
FACTOR = 1.0 / math.sqrt(HEAD_DIM)
F32 = jnp.float32
BF16 = jnp.bfloat16


def bits_of(size):
    bits = []
    while (1 << len(bits)) < size:
        bits.append(1 << len(bits))
    return bits


def swapped(value, axis, bit):
    size = lax.axis_size(axis)
    return lax.ppermute(value, axis, [(i, i ^ bit) for i in range(size)])


def exchanged(near, far, axis):
    size = lax.axis_size(axis)
    pairs = [(i, i ^ 1) for i in range(size) if (i ^ 1) < size]
    others = [(i, i - 1 + 2 * (i % 2)) for i in range(size) if 0 <= i - 1 + 2 * (i % 2) < size]
    return lax.ppermute(near, axis, pairs), lax.ppermute(far, axis, others)


def nt(left, right):
    return lax.dot_general(left, right, (((1,), (1,)), ((), ())), preferred_element_type=F32)


def tn(left, right):
    return lax.dot_general(left, right, (((0,), (0,)), ((), ())), preferred_element_type=F32)


def nn(left, right):
    return jnp.dot(left, right, preferred_element_type=F32)


def inside_band(rows, cols, row_start, col_start, offset, length):
    row_pos = row_start + lax.broadcasted_iota(jnp.int32, (rows, cols), 0)
    col_pos = col_start + lax.broadcasted_iota(jnp.int32, (rows, cols), 1)
    return (
        (jnp.abs(row_pos - col_pos) <= WINDOW)
        & (col_pos + offset >= 0)
        & (col_pos + offset < length)
    )


def pack_kernel(targets, mask, q, k, v, near, far, meta, edges, marks, sems):
    tokens, width = q.shape
    even = lax.rem(lax.axis_index("ctx"), 2) == 0
    edge = 2 * EDGE
    ends = (slice(0, edge), slice(tokens - edge, tokens))
    copies = []

    def fetch(source, target):
        copy = pltpu.make_async_copy(source, target, sems.at[len(copies)])
        copy.start()
        copies.append(copy)

    start = pl.multiple_of(jnp.where(even, tokens - HALO, 0), 16)
    other = pl.multiple_of(jnp.where(even, 0, tokens - HALO), 16)
    for message, first in ((near, start), (far, other)):
        fetch(k.at[pl.ds(first, HALO)], message.at[:, 0:width])
        fetch(v.at[pl.ds(first, HALO)], message.at[:, width : 2 * width])
    for place, end in enumerate(ends):
        fetch(q.at[end], edges.at[place])
    fetch(targets, marks.at[0])
    fetch(mask, marks.at[1])
    for copy in copies[-2:]:
        copy.wait()
    spread = (128, tokens)
    target = jnp.broadcast_to(marks[0], spread).T
    chosen = jnp.broadcast_to(marks[1], spread).T
    spot = lax.broadcasted_iota(jnp.int32, (tokens, 128), 1)
    entry = jnp.where(spot == 0, target >> 5, jnp.where(spot == 1, target & 31, chosen))
    meta[...] = entry.astype(F32)
    for copy in copies[:-2]:
        copy.wait()
    low = lax.broadcasted_iota(jnp.int32, (edge, 1), 0) < EDGE

    def patch(message, place, use, end):
        rows = slice(place, place + edge)
        held = message[rows, :].astype(F32)
        ours = jnp.concatenate(
            [edges[end].astype(F32), meta[ends[end], :], jnp.zeros((edge, width - 128), F32)],
            axis=1,
        )
        ours = jnp.concatenate([ours[EDGE:], ours[:EDGE]], axis=0)
        message[rows, :] = jnp.where(use, ours, held).astype(BF16)

    @pl.when(even)
    def _():
        patch(near, 0, low, 1)
        patch(far, HALO - edge, ~low, 0)

    @pl.when(~even)
    def _():
        patch(near, HALO - edge, ~low, 0)
        patch(far, 0, low, 1)


def stage_kernel(q, k, v, q_own, k_own, v_own):
    q_own[...] = q[...]
    k_own[...] = k[...]
    v_own[...] = v[...]


def attention_kernel(
    info, q, k, v, meta, near, far, attn, lse, k_ext, v_ext, q_ext, meta_ext
):
    tokens, width = q.shape
    length, offset = info[0], info[1]
    even = info[3] == 0
    q_ext[16 : 16 + tokens, :] = q[...]
    k_ext[HALO : HALO + tokens, :] = k[...]
    v_ext[HALO : HALO + tokens, :] = v[...]

    def place_sides(left, right):
        for ext, first in ((k_ext, 0), (v_ext, width)):
            cols = slice(first, first + width)
            ext[0:HALO, :] = left[:, cols]
            ext[HALO + tokens : 2 * HALO + tokens, :] = right[:, cols]
        q_ext[0:16, :] = left[0:16, 0:width]
        q_ext[16 + tokens :, :] = right[HALO - 16 : HALO, 0:width]
        spots = slice(width, width + 128)
        meta_ext[0:EDGE, :] = left[0:16, spots].astype(F32)[0:EDGE]
        meta_ext[EDGE + tokens :, :] = right[HALO - 16 : HALO, spots].astype(F32)[EDGE:]

    @pl.when(even)
    def _():
        place_sides(far, near)

    @pl.when(~even)
    def _():
        place_sides(near, far)

    meta_ext[EDGE : EDGE + tokens, :] = meta[...]
    lse[...] = jnp.zeros(lse.shape, F32)
    rows, span = 16 + WINDOW, 4 * WINDOW
    spot = lax.broadcasted_iota(jnp.int32, (rows, span), 0)
    blocks = [
        (0, 0, jnp.where(spot < EDGE, spot - EDGE, spot - 16)),
        (
            tokens + 32 - rows,
            tokens + 2 * HALO - span,
            jnp.where(spot < WINDOW, spot + tokens - WINDOW, spot + tokens - WINDOW - EDGE),
        ),
    ]
    for place, key_row, query_pos in blocks:
        key_pos = key_row - HALO + lax.broadcasted_iota(jnp.int32, (rows, span), 1)
        inside = (
            (jnp.abs(query_pos - key_pos) <= WINDOW)
            & (key_pos + offset >= 0)
            & (key_pos + offset < length)
        )
        keys = slice(key_row, key_row + span)
        first = max(place, 16)
        own = slice(first - place, first - place + WINDOW)
        for at in range(0, width, HEAD_DIM):
            cols = slice(at, at + HEAD_DIM)
            head = at // HEAD_DIM
            scores = nt(q_ext[place : place + rows, cols], k_ext[keys, cols]) * FACTOR
            scores = jnp.where(inside, scores, LOW)
            top = jnp.max(scores, axis=-1, keepdims=True)
            grown = jnp.exp(scores - top)
            total = jnp.sum(grown, axis=-1, keepdims=True)
            mixed = nn(grown.astype(BF16), v_ext[keys, cols]) * (1.0 / total)
            attn[place : place + rows, cols] = mixed.astype(BF16)
            level = top + jnp.log(total)
            lse[first - 16 : first - 16 + WINDOW, 4 + head : 5 + head] = level[own]


def middle_kernel(marks, info, attn, lse, meta_ext, taps, *refs):
    count = len(marks)
    out_parts, head_parts = refs[:count], refs[count : 2 * count]
    d_attn, stats, summary = refs[2 * count : 2 * count + 3]
    (
        out_full, head_full, hid, gated, slope, logits, d_logits, d_pre, d_hid, sems,
    ) = refs[2 * count + 3 :]
    length, offset, mine = info[0], info[1], info[2]
    copies = []
    for parts, full in ((out_parts, out_full), (head_parts, head_full)):
        for mark, part in zip(marks, parts):
            rows = part.shape[0]
            start = pl.multiple_of((mine ^ mark) * rows, rows)
            copy = pltpu.make_async_copy(part, full.at[pl.ds(start, rows)], sems.at[len(copies)])
            copy.start()
            copies.append(copy)
    tokens, width = d_attn.shape
    depth = out_full.shape[1]
    vocab = head_full.shape[1]
    ext = tokens + 2 * EDGE
    lanes = 128

    row_pos = offset - EDGE + lax.broadcasted_iota(jnp.int32, (ext, lanes), 0)
    live = (row_pos >= 0) & (row_pos < length)
    hid[:, 0:EDGE, :] = jnp.zeros((depth // lanes, EDGE, lanes), F32)
    hid[:, EDGE + ext :, :] = jnp.zeros((depth // lanes, EDGE, lanes), F32)
    for copy in copies[:count]:
        copy.wait()
    for at in range(0, depth, 256):
        block = nn(attn[...], out_full[:, at : at + 256])
        block = jnp.concatenate(
            [block[0:EDGE], block[16 : 16 + tokens], block[16 + tokens + EDGE :]], axis=0
        )
        for part in range(2):
            piece = block[:, part * lanes : (part + 1) * lanes]
            hid[at // lanes + part, EDGE : EDGE + ext, :] = jnp.where(live, piece, 0.0)
    for chunk in range(depth // lanes):
        cols = slice(chunk * lanes, (chunk + 1) * lanes)
        conv = jnp.zeros((ext, lanes), F32)
        for tap in range(TAPS):
            start = EDGE - MARGIN + tap
            conv = conv + taps[tap : tap + 1, cols] * hid[chunk, start : start + ext, :]
        sigma = jax.nn.sigmoid(conv)
        gated[:, cols] = (conv * sigma).astype(BF16)
        slope[chunk] = sigma * (1.0 + conv * (1.0 - sigma))
    for copy in copies[count:]:
        copy.wait()
    for at in range(0, vocab, 256):
        logits[:, at : at + 256] = nn(gated[...], head_full[:, at : at + 256])

    meta_all = meta_ext[...]
    target = (meta_all[:, 0:1] * 32.0 + meta_all[:, 1:2]).astype(jnp.int32)
    chosen = jnp.where(live & (meta_all[:, 2:3] == 1.0), 1.0, 0.0)[:, 0:1]
    loss_rows = jnp.zeros((16, 1), F32)
    count_rows = jnp.zeros((16, 1), F32)
    word = lax.broadcasted_iota(jnp.int32, (16, vocab), 1)
    row_in = lax.broadcasted_iota(jnp.int32, (16, 1), 0)
    for at in range(0, ext, 16):
        block = logits[at : at + 16, :]
        top = jnp.max(block, axis=-1, keepdims=True)
        grown = jnp.exp(block - top)
        total = jnp.sum(grown, axis=-1, keepdims=True)
        hit = target[at : at + 16] == word
        picked = jnp.sum(jnp.where(hit, block, 0.0), axis=-1, keepdims=True)
        pick = chosen[at : at + 16]
        change = grown * (pick / total) - jnp.where(hit, pick, 0.0)
        d_logits[at : at + 16, :] = change.astype(BF16)
        own = (row_in + at >= EDGE) & (row_in + at < EDGE + tokens)
        kept = jnp.where(own, pick, 0.0)
        loss_rows = loss_rows + kept * (top + jnp.log(total) - picked)
        count_rows = count_rows + kept
    summary[...] = jnp.zeros(summary.shape, F32)
    lane = lax.broadcasted_iota(jnp.int32, (1, lanes), 1)
    loss_sum = jnp.sum(loss_rows, axis=0, keepdims=True)
    count_sum = jnp.sum(count_rows, axis=0, keepdims=True)
    summary[TAPS : TAPS + 1, 0:lanes] = jnp.where(
        lane == 0, loss_sum, jnp.where(lane == 1, count_sum, 0.0)
    )
    for at in range(0, depth, 256):
        d_gated = nt(d_logits[...], head_full[at : at + 256, :])
        for part in range(2):
            chunk = at // lanes + part
            cols = slice(chunk * lanes, (chunk + 1) * lanes)
            change = d_gated[:, part * lanes : (part + 1) * lanes] * slope[chunk]
            d_pre[chunk] = change
            owned = change[EDGE : EDGE + tokens]
            for tap in range(TAPS):
                start = 2 * EDGE - MARGIN + tap
                summary[tap : tap + 1, cols] = jnp.sum(
                    owned * hid[chunk, start : start + tokens, :], axis=0, keepdims=True
                )
    for chunk in range(depth // lanes):
        cols = slice(chunk * lanes, (chunk + 1) * lanes)
        change = jnp.zeros((tokens, lanes), F32)
        for tap in range(TAPS):
            start = EDGE + MARGIN - tap
            change = change + taps[tap : tap + 1, cols] * d_pre[chunk, start : start + tokens, :]
        d_hid[:, cols] = jnp.where(live[EDGE : EDGE + tokens], change, 0.0).astype(BF16)
    stats[...] = lse[...]
    for at in range(0, width, HEAD_DIM):
        cols = slice(at, at + HEAD_DIM)
        head = at // HEAD_DIM
        block = nt(d_hid[...], out_full[cols, :]).astype(BF16)
        d_attn[:, cols] = block
        products = block.astype(F32) * attn[16 : 16 + tokens, cols].astype(F32)
        stats[:, head : head + 1] = jnp.sum(products, axis=-1, keepdims=True)


def edge_grads_kernel(info, q_ext, k_ext, v_ext, stats, d_attn, near, far):
    tokens, width = d_attn.shape
    length, offset = info[0], info[1]
    even = info[3] == 0
    for out, on_right in ((near, even), (far, ~even)):
        first = pl.multiple_of(jnp.where(on_right, tokens - WINDOW, 0), WINDOW)
        key_start = jnp.where(on_right, tokens, -WINDOW)
        rows = pl.ds(first, WINDOW)
        asked = pl.ds(pl.multiple_of(first + 16, 16), WINDOW)
        keys = pl.ds(pl.multiple_of(key_start + HALO, 16), WINDOW)
        by_row = stats[rows, :].T
        key_pos = key_start + lax.broadcasted_iota(jnp.int32, (WINDOW, WINDOW), 0)
        query_pos = first + lax.broadcasted_iota(jnp.int32, (WINDOW, WINDOW), 1)
        inside = (
            (jnp.abs(query_pos - key_pos) <= WINDOW)
            & (key_pos + offset >= 0)
            & (key_pos + offset < length)
        )
        for start in range(0, width, HEAD_DIM):
            cols = slice(start, start + HEAD_DIM)
            head = start // HEAD_DIM
            query, change = q_ext[asked, cols], d_attn[rows, cols]
            scores = jnp.where(inside, nt(k_ext[keys, cols], query) * FACTOR, LOW)
            probs = jnp.exp(scores - by_row[4 + head : 5 + head, :])
            d_scores = probs * (nt(v_ext[keys, cols], change) - by_row[head : head + 1, :])
            out[:, cols] = (nn(d_scores.astype(BF16), query) * FACTOR).astype(BF16)
            out[:, width + start : width + start + HEAD_DIM] = nn(
                probs.astype(BF16), change
            ).astype(BF16)


def own_grads_kernel(info, q_ext, k_ext, v_ext, stats, d_attn, d_q, d_k, d_v):
    tokens, width = d_attn.shape
    length, offset = info[0], info[1]
    span = 3 * WINDOW
    d_k[...] = jnp.zeros(d_k.shape, F32)
    d_v[...] = jnp.zeros(d_v.shape, F32)
    for at in range(0, tokens, WINDOW):
        rows = slice(at, at + WINDOW)
        key_row = HALO - WINDOW + at
        inside = inside_band(WINDOW, span, at, at - WINDOW, offset, length)
        first = max(at - WINDOW, 0)
        last = min(at + 2 * WINDOW, tokens)
        mine = slice(first - at + WINDOW, last - at + WINDOW)
        for start in range(0, width, HEAD_DIM):
            cols = slice(start, start + HEAD_DIM)
            head = start // HEAD_DIM
            query, change = q_ext[at + 16 : at + 16 + WINDOW, cols], d_attn[rows, cols]
            keys = k_ext[key_row : key_row + span, cols]
            values = v_ext[key_row : key_row + span, cols]
            scores = jnp.where(inside, nt(query, keys) * FACTOR, LOW)
            probs = jnp.exp(scores - stats[rows, 4 + head : 5 + head])
            d_scores = probs * (nt(change, values) - stats[rows, head : head + 1])
            d_scores = d_scores.astype(BF16)
            d_q[rows, cols] = (nn(d_scores, keys) * FACTOR).astype(BF16)
            d_k[first:last, cols] += tn(d_scores[:, mine], query) * FACTOR
            d_v[first:last, cols] += tn(probs.astype(BF16)[:, mine], change)


def add_kernel(info, k_part, v_part, near, far, d_k, d_v):
    tokens, width = d_k.shape
    even = info[3] == 0
    for got, on_right in ((near, even), (far, ~even)):
        rows = pl.ds(pl.multiple_of(jnp.where(on_right, tokens - WINDOW, 0), WINDOW), WINDOW)
        for out, part, cols in (
            (d_k, k_part, slice(0, width)),
            (d_v, v_part, slice(width, 2 * width)),
        ):
            out[rows, :] = (part[rows, :] + got[0:WINDOW, cols].astype(F32)).astype(BF16)


def grouped(bits):
    pairs = [bits[at : at + 2] for at in range(0, len(bits), 2)]
    return [pair + [pair[0] ^ pair[1]] if len(pair) == 2 else pair for pair in pairs]


def packed(totals):
    rounded = lax.reduce_precision(totals[:TAPS], 8, 7)
    first = lax.reduce_precision(totals[TAPS:], 8, 7)
    second = lax.reduce_precision(totals[TAPS:] - first, 8, 7)
    third = totals[TAPS:] - first - second
    return jnp.concatenate([rounded, first, second, third], axis=0).astype(BF16)


def unpacked(sent):
    wide = sent.astype(F32)
    last = wide[TAPS : TAPS + 1] + wide[TAPS + 1 : TAPS + 2] + wide[TAPS + 2 : TAPS + 3]
    return jnp.concatenate([wide[:TAPS], last], axis=0)


def added(parts):
    sums = [unpacked(part) for part in parts]
    while len(sums) > 1:
        sums = [sums[at] + sums[at + 1] for at in range(0, len(sums), 2)]
    return sums[0]


def finish_kernel(*refs):
    parts, (d_conv, loss) = refs[:-2], refs[-2:]
    taps = [part[...].astype(F32)[0:TAPS] for part in parts]
    sums = []
    for part in parts:
        wide = part[...].astype(F32)
        sums.append(wide[TAPS : TAPS + 1] + wide[TAPS + 1 : TAPS + 2] + wide[TAPS + 2 : TAPS + 3])
    while len(taps) > 1:
        taps = [taps[at] + taps[at + 1] for at in range(0, len(taps), 2)]
        sums = [sums[at] + sums[at + 1] for at in range(0, len(sums), 2)]
    count = sums[0][:, 1:2]
    d_conv[...] = taps[0] / jnp.sqrt(count)
    loss[...] = sums[0][:, 0:1] / count


def call(kernel, operands, outs, scratch, places, flops, limit=24):
    specs = {
        "s": pl.BlockSpec(memory_space=pltpu.SMEM),
        "v": pl.BlockSpec(memory_space=pltpu.VMEM),
        "a": pl.BlockSpec(memory_space=pl.ANY),
    }
    arrays = list(operands) + list(outs)
    size = sum(math.prod(item.shape) * item.dtype.itemsize for item in arrays) if flops else 1
    return pl.pallas_call(
        kernel,
        out_shape=outs,
        in_specs=[specs[place] for place in places],
        out_specs=[specs["v"] for _ in outs],
        scratch_shapes=scratch,
        compiler_params=pltpu.CompilerParams(vmem_limit_bytes=limit * 1024 * 1024),
        cost_estimate=pl.CostEstimate(flops=max(flops, 1), bytes_accessed=size, transcendentals=0),
    )(*operands)


def local(
    queries,
    key_rows,
    value_rows,
    out_weight,
    head_weight,
    conv_weight,
    lengths,
    label_mask,
    targets,
):
    tokens, width = queries.shape[1:]
    depth = out_weight.shape[1]
    vocab = head_weight.shape[1]
    dp_size = lax.axis_size("dp")
    place = lax.axis_index("ctx")
    q, k, v = queries[0], key_rows[0], value_rows[0]
    info = jnp.stack([lengths[0], place * tokens, lax.axis_index("dp"), place % 2])
    info = info.astype(jnp.int32)

    shape = jax.ShapeDtypeStruct
    halo = shape((HALO, 2 * width), BF16)
    block = shape((tokens, width), BF16)
    near, far, meta = call(
        pack_kernel,
        (targets, label_mask, q, k, v),
        (halo, halo, shape((tokens, 128), F32)),
        [
            pltpu.VMEM((2, 2 * EDGE, width), BF16),
            pltpu.VMEM((2, 1, tokens), jnp.int32),
            pltpu.SemaphoreType.DMA((8,)),
        ],
        "aaaaa",
        0,
        56,
    )
    q_own, k_own, v_own = call(stage_kernel, (q, k, v), (block, block, block), [], "vvv", 0)
    near, far = exchanged(near, far, "ctx")
    ext = tokens + 2 * EDGE
    attn, lse, k_ext, v_ext, q_ext, meta_ext = call(
        attention_kernel,
        (info, q_own, k_own, v_own, meta, near, far),
        (
            shape((tokens + 32, width), BF16),
            shape((tokens, 128), F32),
            shape((tokens + 2 * HALO, width), BF16),
            shape((tokens + 2 * HALO, width), BF16),
            shape((tokens + 32, width), BF16),
            shape((ext, 128), F32),
        ),
        [],
        "svvvvvv",
        4 * tokens * 3 * WINDOW * width,
    )
    top_bit = bits_of(dp_size)[-1]
    first_hop = [swapped(head_weight, "dp", top_bit), swapped(out_weight, "dp", top_bit)]
    attn, head_far, out_far = lax.optimization_barrier((attn, *first_hop))
    held, marks = [], []
    for weight, received in ((out_weight, out_far), (head_weight, head_far)):
        pieces = [(0, weight), (top_bit, received)]
        for bit in reversed(bits_of(dp_size)[:-1]):
            pieces += [(mark ^ bit, swapped(item, "dp", bit)) for mark, item in pieces]
        marks = [mark for mark, _ in pieces]
        held += [item for _, item in pieces]

    chunks = depth // 128
    d_attn, stats, summary = call(
        functools.partial(middle_kernel, tuple(marks)),
        (info, attn, lse, meta_ext, conv_weight, *held),
        (
            shape((tokens, width), BF16),
            shape((tokens, 128), F32),
            shape((16, depth), F32),
        ),
        [
            pltpu.VMEM((width, depth), BF16),
            pltpu.VMEM((depth, vocab), BF16),
            pltpu.VMEM((chunks, ext + 2 * EDGE, 128), F32),
            pltpu.VMEM((ext, depth), BF16),
            pltpu.VMEM((chunks, ext, 128), F32),
            pltpu.VMEM((ext, vocab), F32),
            pltpu.VMEM((ext, vocab), BF16),
            pltpu.VMEM((chunks, ext, 128), F32),
            pltpu.VMEM((tokens, depth), BF16),
            pltpu.SemaphoreType.DMA((2 * dp_size,)),
        ],
        "svvvv" + "a" * (2 * dp_size),
        4 * tokens * depth * (width + vocab),
    )

    totals = summary[: TAPS + 1]
    dp_bits, ctx_bits = bits_of(dp_size), bits_of(lax.axis_size("ctx"))
    near_part, far_part = call(
        edge_grads_kernel,
        (info, q_ext, k_ext, v_ext, stats, d_attn),
        (shape((WINDOW, 2 * width), BF16), shape((WINDOW, 2 * width), BF16)),
        [],
        "svvvvv",
        16 * WINDOW * WINDOW * width,
    )
    for index, group in enumerate(grouped(dp_bits)):
        sent = packed(totals)
        got = [swapped(sent, "dp", bit) for bit in group]
        if index == 0:
            near_part, far_part, *got = lax.optimization_barrier((near_part, far_part, *got))
        totals = added([sent] + got)
    sent = packed(totals)
    near_part = jnp.concatenate([near_part, sent], axis=0)
    near_got, far_got = exchanged(near_part, far_part, "ctx")
    d_q, k_part, v_part = call(
        own_grads_kernel,
        (info, q_ext, k_ext, v_ext, stats, d_attn),
        (block, shape((tokens, width), F32), shape((tokens, width), F32)),
        [],
        "svvvvv",
        10 * tokens * 3 * WINDOW * width,
    )
    near_got, d_q, k_part, v_part = lax.optimization_barrier((near_got, d_q, k_part, v_part))
    totals = added([sent, near_got[WINDOW:]])
    groups = grouped(ctx_bits[1:])
    for index, group in enumerate(groups):
        sent = packed(totals)
        got = [swapped(sent, "ctx", bit) for bit in group]
        if index < len(groups) - 1:
            totals = added([sent] + got)
    d_k, d_v = call(
        add_kernel,
        (info, k_part, v_part, near_got, far_got),
        (block, block),
        [],
        "svvvv",
        tokens * width,
    )
    d_k, d_v, *got = lax.optimization_barrier((d_k, d_v, *got))
    d_conv, loss = call(
        finish_kernel,
        (sent, *got),
        (shape((TAPS, depth), F32), shape((1, 1), F32)),
        [],
        "v" * (1 + len(got)),
        0,
    )
    return (loss[0, 0], d_q[None], d_k[None], d_v[None], d_conv)


def solution(mesh):
    placed = (
        P("dp", "ctx", None),
        P("dp", "ctx", None),
        P("dp", "ctx", None),
        P("dp", None),
        P("dp", None),
        P(),
        P("dp"),
        P("dp", "ctx"),
        P("dp", "ctx"),
    )
    return jax.shard_map(
        local,
        mesh=mesh,
        in_specs=placed,
        out_specs=(P(), P("dp", "ctx", None), P("dp", "ctx", None), P("dp", "ctx", None), P()),
        check_vma=False,
    )
```

```python
import functools
import math

import jax
import jax.numpy as jnp
from jax import lax
from jax.experimental import pallas as pl
from jax.experimental.pallas import tpu as pltpu
from jax.sharding import PartitionSpec as P

HEAD_DIM = 128
WINDOW = 128
TAPS = 9
MARGIN = (TAPS - 1) // 2
EDGE = 8
HALO = WINDOW + 2 * EDGE
LOW = -1e30
FACTOR = 1.0 / math.sqrt(HEAD_DIM)
F32 = jnp.float32
BF16 = jnp.bfloat16


def bits_of(size):
    bits = []
    while (1 << len(bits)) < size:
        bits.append(1 << len(bits))
    return bits


def swapped(value, axis, bit):
    size = lax.axis_size(axis)
    return lax.ppermute(value, axis, [(i, i ^ bit) for i in range(size)])


def exchanged(near, far, axis):
    size = lax.axis_size(axis)
    pairs = [(i, i ^ 1) for i in range(size) if (i ^ 1) < size]
    others = [(i, i - 1 + 2 * (i % 2)) for i in range(size) if 0 <= i - 1 + 2 * (i % 2) < size]
    return lax.ppermute(near, axis, pairs), lax.ppermute(far, axis, others)


def nt(left, right):
    return lax.dot_general(left, right, (((1,), (1,)), ((), ())), preferred_element_type=F32)


def tn(left, right):
    return lax.dot_general(left, right, (((0,), (0,)), ((), ())), preferred_element_type=F32)


def nn(left, right):
    return jnp.dot(left, right, preferred_element_type=F32)


def in_reach(query_pos, key_pos, offset, length):
    return (
        (jnp.abs(query_pos - key_pos) <= WINDOW)
        & (key_pos + offset >= 0)
        & (key_pos + offset < length)
    )


def pack_kernel(targets, mask, q, k, v, head, near, far, meta, piece, edges, marks, sems):
    tokens, width = q.shape
    half = piece.shape[0]
    even = lax.rem(lax.axis_index("ctx"), 2) == 0
    edge = 2 * EDGE
    ends = (slice(0, edge), slice(tokens - edge, tokens))
    copies = []

    def fetch(source, target):
        copy = pltpu.make_async_copy(source, target, sems.at[len(copies)])
        copy.start()
        copies.append(copy)

    start = pl.multiple_of(jnp.where(even, tokens - HALO, 0), 16)
    other = pl.multiple_of(jnp.where(even, 0, tokens - HALO), 16)
    for message, first in ((near, start), (far, other)):
        fetch(k.at[pl.ds(first, HALO)], message.at[:, 0:width])
        fetch(v.at[pl.ds(first, HALO)], message.at[:, width : 2 * width])
    for place, end in enumerate(ends):
        fetch(q.at[end], edges.at[place])
    start = pl.multiple_of(lax.rem(lax.axis_index("ctx") // 2, 2) * half, half)
    fetch(head.at[pl.ds(start, half)], piece)
    fetch(targets, marks.at[0])
    fetch(mask, marks.at[1])
    for copy in copies[-2:]:
        copy.wait()
    spread = (128, tokens)
    target = jnp.broadcast_to(marks[0], spread).T
    chosen = jnp.broadcast_to(marks[1], spread).T
    spot = lax.broadcasted_iota(jnp.int32, (tokens, 128), 1)
    entry = jnp.where(spot == 0, target >> 5, jnp.where(spot == 1, target & 31, chosen))
    meta[...] = entry.astype(F32)
    for copy in copies[:-2]:
        copy.wait()
    low = lax.broadcasted_iota(jnp.int32, (edge, 1), 0) < EDGE

    def patch(message, place, use, end):
        rows = slice(place, place + edge)
        held = message[rows, :].astype(F32)
        ours = jnp.concatenate(
            [edges[end].astype(F32), meta[ends[end], :], jnp.zeros((edge, width - 128), F32)],
            axis=1,
        )
        ours = jnp.concatenate([ours[EDGE:], ours[:EDGE]], axis=0)
        message[rows, :] = jnp.where(use, ours, held).astype(BF16)

    @pl.when(even)
    def _():
        patch(near, 0, low, 1)
        patch(far, HALO - edge, ~low, 0)

    @pl.when(~even)
    def _():
        patch(near, HALO - edge, ~low, 0)
        patch(far, 0, low, 1)


def stage_kernel(q, k, v, q_own, k_own, v_own):
    q_own[...] = q[...]
    k_own[...] = k[...]
    v_own[...] = v[...]


def attention_kernel(
    info, q, k, v, meta, near, far, attn, lse, k_ext, v_ext, q_ext, meta_ext
):
    tokens, width = q.shape
    length, offset = info[0], info[1]
    even = info[3] == 0
    q_ext[16 : 16 + tokens, :] = q[...]
    k_ext[HALO : HALO + tokens, :] = k[...]
    v_ext[HALO : HALO + tokens, :] = v[...]

    def place_sides(left, right):
        for ext, first in ((k_ext, 0), (v_ext, width)):
            cols = slice(first, first + width)
            ext[0:HALO, :] = left[:, cols]
            ext[HALO + tokens : 2 * HALO + tokens, :] = right[:, cols]
        q_ext[0:16, :] = left[0:16, 0:width]
        q_ext[16 + tokens :, :] = right[HALO - 16 : HALO, 0:width]
        spots = slice(width, width + 128)
        meta_ext[0:EDGE, :] = left[0:16, spots].astype(F32)[0:EDGE]
        meta_ext[EDGE + tokens :, :] = right[HALO - 16 : HALO, spots].astype(F32)[EDGE:]

    @pl.when(even)
    def _():
        place_sides(far, near)

    @pl.when(~even)
    def _():
        place_sides(near, far)

    meta_ext[EDGE : EDGE + tokens, :] = meta[...]
    lse[...] = jnp.zeros(lse.shape, F32)
    rows, span = 16 + WINDOW, 4 * WINDOW
    spot = lax.broadcasted_iota(jnp.int32, (rows, span), 0)
    blocks = [
        (0, 0, jnp.where(spot < EDGE, spot - EDGE, spot - 16)),
        (
            tokens + 32 - rows,
            tokens + 2 * HALO - span,
            jnp.where(spot < WINDOW, spot + tokens - WINDOW, spot + tokens - WINDOW - EDGE),
        ),
    ]
    work = []
    for place, key_row, query_pos in blocks:
        key_pos = key_row - HALO + lax.broadcasted_iota(jnp.int32, (rows, span), 1)
        inside = in_reach(query_pos, key_pos, offset, length)
        keys = slice(key_row, key_row + span)
        work += [(place, keys, inside, at) for at in range(0, width, HEAD_DIM)]

    def scores_of(item):
        place, keys, inside, at = item
        cols = slice(at, at + HEAD_DIM)
        product = nt(q_ext[place : place + rows, cols], k_ext[keys, cols])
        return jnp.where(inside, product * FACTOR, LOW)

    scores = scores_of(work[0])
    for index, (place, keys, _, at) in enumerate(work):
        later = scores_of(work[index + 1]) if index + 1 < len(work) else None
        cols = slice(at, at + HEAD_DIM)
        head = at // HEAD_DIM
        top = jnp.max(scores, axis=-1, keepdims=True)
        grown = jnp.exp(scores - top)
        total = jnp.sum(grown, axis=-1, keepdims=True)
        mixed = nn(grown.astype(BF16), v_ext[keys, cols]) * (1.0 / total)
        attn[place : place + rows, cols] = mixed.astype(BF16)
        level = top + jnp.log(total)
        first = max(place, 16)
        lse[first - 16 : first - 16 + WINDOW, 4 + head : 5 + head] = level[
            first - place : first - place + WINDOW
        ]
        scores = later


def middle_kernel(marks, info, attn, lse, meta_ext, taps, *refs):
    count = sum(len(pieces) for pieces in marks)
    held = list(refs[:count])
    d_attn, stats, summary = refs[count : count + 3]
    (
        out_full, head_full, hid, gated, slope, logits, d_logits, d_pre, d_hid, sems,
    ) = refs[count + 3 :]
    length, offset, mine = info[0], info[1], info[2]
    copies = []
    for full, pieces, halves in ((out_full, marks[0], 1), (head_full, marks[1], 1), (head_full, marks[2], 2)):
        for mark, part in pieces:
            source = held[len(copies)]
            rows = source.shape[0]
            start = (mine ^ mark) * (rows * halves)
            if halves == 2:
                start = start + (info[4] ^ part) * rows
            target = full.at[pl.ds(pl.multiple_of(start, rows), rows)]
            copy = pltpu.make_async_copy(source, target, sems.at[len(copies)])
            copy.start()
            copies.append(copy)
    tokens, width = d_attn.shape
    depth = out_full.shape[1]
    vocab = head_full.shape[1]
    ext = tokens + 2 * EDGE
    lanes = 128

    row_pos = offset - EDGE + lax.broadcasted_iota(jnp.int32, (ext, lanes), 0)
    live = (row_pos >= 0) & (row_pos < length)
    hid[:, 0:EDGE, :] = jnp.zeros((depth // lanes, EDGE, lanes), F32)
    hid[:, EDGE + ext :, :] = jnp.zeros((depth // lanes, EDGE, lanes), F32)
    for copy in copies[: len(marks[0])]:
        copy.wait()
    for at in range(0, depth, 256):
        block = nn(attn[...], out_full[:, at : at + 256])
        block = jnp.concatenate(
            [block[0:EDGE], block[16 : 16 + tokens], block[16 + tokens + EDGE :]], axis=0
        )
        for part in range(2):
            piece = block[:, part * lanes : (part + 1) * lanes]
            hid[at // lanes + part, EDGE : EDGE + ext, :] = jnp.where(live, piece, 0.0)
    for chunk in range(depth // lanes):
        cols = slice(chunk * lanes, (chunk + 1) * lanes)
        conv = jnp.zeros((ext, lanes), F32)
        for tap in range(TAPS):
            start = EDGE - MARGIN + tap
            conv = conv + taps[tap : tap + 1, cols] * hid[chunk, start : start + ext, :]
        sigma = jax.nn.sigmoid(conv)
        gated[:, cols] = (conv * sigma).astype(BF16)
        slope[chunk] = sigma * (1.0 + conv * (1.0 - sigma))
    for copy in copies[len(marks[0]) :]:
        copy.wait()
    for at in range(0, vocab, 256):
        logits[:, at : at + 256] = nn(gated[...], head_full[:, at : at + 256])

    meta_all = meta_ext[...]
    target = (meta_all[:, 0:1] * 32.0 + meta_all[:, 1:2]).astype(jnp.int32)
    chosen = jnp.where(live & (meta_all[:, 2:3] == 1.0), 1.0, 0.0)[:, 0:1]
    loss_rows = jnp.zeros((16, 1), F32)
    count_rows = jnp.zeros((16, 1), F32)
    word = lax.broadcasted_iota(jnp.int32, (16, vocab), 1)
    row_in = lax.broadcasted_iota(jnp.int32, (16, 1), 0)
    for at in range(0, ext, 16):
        block = logits[at : at + 16, :]
        top = jnp.max(block, axis=-1, keepdims=True)
        grown = jnp.exp(block - top)
        total = jnp.sum(grown, axis=-1, keepdims=True)
        hit = target[at : at + 16] == word
        picked = jnp.sum(jnp.where(hit, block, 0.0), axis=-1, keepdims=True)
        pick = chosen[at : at + 16]
        change = grown * (pick / total) - jnp.where(hit, pick, 0.0)
        d_logits[at : at + 16, :] = change.astype(BF16)
        own = (row_in + at >= EDGE) & (row_in + at < EDGE + tokens)
        kept = jnp.where(own, pick, 0.0)
        loss_rows = loss_rows + kept * (top + jnp.log(total) - picked)
        count_rows = count_rows + kept
    summary[...] = jnp.zeros(summary.shape, F32)
    lane = lax.broadcasted_iota(jnp.int32, (1, lanes), 1)
    loss_sum = jnp.sum(loss_rows, axis=0, keepdims=True)
    count_sum = jnp.sum(count_rows, axis=0, keepdims=True)
    summary[TAPS : TAPS + 1, 0:lanes] = jnp.where(
        lane == 0, loss_sum, jnp.where(lane == 1, count_sum, 0.0)
    )
    for at in range(0, depth, 256):
        d_gated = nt(d_logits[...], head_full[at : at + 256, :])
        for part in range(2):
            chunk = at // lanes + part
            cols = slice(chunk * lanes, (chunk + 1) * lanes)
            change = d_gated[:, part * lanes : (part + 1) * lanes] * slope[chunk]
            d_pre[chunk] = change
            owned = change[EDGE : EDGE + tokens]
            for tap in range(TAPS):
                start = 2 * EDGE - MARGIN + tap
                summary[tap : tap + 1, cols] = jnp.sum(
                    owned * hid[chunk, start : start + tokens, :], axis=0, keepdims=True
                )
    for chunk in range(depth // lanes):
        cols = slice(chunk * lanes, (chunk + 1) * lanes)
        change = jnp.zeros((tokens, lanes), F32)
        for tap in range(TAPS):
            start = EDGE + MARGIN - tap
            change = change + taps[tap : tap + 1, cols] * d_pre[chunk, start : start + tokens, :]
        d_hid[:, cols] = jnp.where(live[EDGE : EDGE + tokens], change, 0.0).astype(BF16)
    stats[...] = lse[...]
    for at in range(0, width, HEAD_DIM):
        cols = slice(at, at + HEAD_DIM)
        head = at // HEAD_DIM
        block = nt(d_hid[...], out_full[cols, :]).astype(BF16)
        d_attn[:, cols] = block
        products = block.astype(F32) * attn[16 : 16 + tokens, cols].astype(F32)
        stats[:, head : head + 1] = jnp.sum(products, axis=-1, keepdims=True)


def edge_grads_kernel(info, q_ext, k_ext, v_ext, stats, d_attn, near, far):
    tokens, width = d_attn.shape
    length, offset = info[0], info[1]
    even = info[3] == 0
    work = []
    for out, on_right in ((near, even), (far, ~even)):
        first = pl.multiple_of(jnp.where(on_right, tokens - WINDOW, 0), WINDOW)
        key_start = jnp.where(on_right, tokens, -WINDOW)
        rows = pl.ds(first, WINDOW)
        asked = pl.ds(pl.multiple_of(first + 16, 16), WINDOW)
        keys = pl.ds(pl.multiple_of(key_start + HALO, 16), WINDOW)
        by_row = stats[rows, :].T
        key_pos = key_start + lax.broadcasted_iota(jnp.int32, (WINDOW, WINDOW), 0)
        query_pos = first + lax.broadcasted_iota(jnp.int32, (WINDOW, WINDOW), 1)
        inside = in_reach(query_pos, key_pos, offset, length)
        for head in range(width // HEAD_DIM):
            cols = slice(head * HEAD_DIM, (head + 1) * HEAD_DIM)
            query, change = q_ext[asked, cols], d_attn[rows, cols]
            scores = jnp.where(inside, nt(k_ext[keys, cols], query) * FACTOR, LOW)
            d_probs = nt(v_ext[keys, cols], change)
            work.append((out, head, by_row, query, change, scores, d_probs))
    done = []
    for out, head, by_row, query, change, scores, d_probs in work:
        probs = jnp.exp(scores - by_row[4 + head : 5 + head, :])
        d_scores = probs * (d_probs - by_row[head : head + 1, :])
        done.append((out, head, query, change, d_scores.astype(BF16), probs.astype(BF16)))
    for out, head, query, change, d_scores, probs in done:
        cols = slice(head * HEAD_DIM, (head + 1) * HEAD_DIM)
        out[:, cols] = (nn(d_scores, query) * FACTOR).astype(BF16)
        cols = slice(width + head * HEAD_DIM, width + (head + 1) * HEAD_DIM)
        out[:, cols] = nn(probs, change).astype(BF16)


def own_grads_kernel(info, q_ext, k_ext, v_ext, stats, d_attn, d_q, d_k, d_v):
    tokens, width = d_attn.shape
    length, offset = info[0], info[1]
    span = tokens + 2 * WINDOW
    keys = slice(HALO - WINDOW, HALO + tokens + WINDOW)
    own = slice(WINDOW, WINDOW + tokens)
    by_row = stats[...].T
    key_pos = lax.broadcasted_iota(jnp.int32, (span, tokens), 0) - WINDOW
    query_pos = lax.broadcasted_iota(jnp.int32, (span, tokens), 1)
    inside = in_reach(query_pos, key_pos, offset, length)

    def products_of(head):
        cols = slice(head * HEAD_DIM, (head + 1) * HEAD_DIM)
        scores = nt(k_ext[keys, cols], q_ext[16 : 16 + tokens, cols])
        return jnp.where(inside, scores * FACTOR, LOW), nt(v_ext[keys, cols], d_attn[:, cols])

    heads = width // HEAD_DIM
    products = products_of(0)
    for head in range(heads):
        later = products_of(head + 1) if head + 1 < heads else None
        cols = slice(head * HEAD_DIM, (head + 1) * HEAD_DIM)
        scores, d_probs = products
        probs = jnp.exp(scores - by_row[4 + head : 5 + head, :])
        d_scores = (probs * (d_probs - by_row[head : head + 1, :])).astype(BF16)
        d_k[:, cols] = nn(d_scores[own], q_ext[16 : 16 + tokens, cols]) * FACTOR
        d_v[:, cols] = nn(probs[own].astype(BF16), d_attn[:, cols])
        d_q[:, cols] = (tn(k_ext[keys, cols], d_scores) * FACTOR).T.astype(BF16)
        products = later


def add_kernel(info, k_part, v_part, near, far, d_k, d_v):
    tokens, width = d_k.shape
    even = info[3] == 0
    for got, on_right in ((near, even), (far, ~even)):
        rows = pl.ds(pl.multiple_of(jnp.where(on_right, tokens - WINDOW, 0), WINDOW), WINDOW)
        for out, part, cols in (
            (d_k, k_part, slice(0, width)),
            (d_v, v_part, slice(width, 2 * width)),
        ):
            out[rows, :] = (part[rows, :] + got[0:WINDOW, cols].astype(F32)).astype(BF16)


def grouped(bits):
    pairs = [bits[at : at + 2] for at in range(0, len(bits), 2)]
    return [pair + [pair[0] ^ pair[1]] if len(pair) == 2 else pair for pair in pairs]


def packed(totals):
    rounded = lax.reduce_precision(totals[:TAPS], 8, 7)
    first = lax.reduce_precision(totals[TAPS:], 8, 7)
    second = lax.reduce_precision(totals[TAPS:] - first, 8, 7)
    third = totals[TAPS:] - first - second
    return jnp.concatenate([rounded, first, second, third], axis=0).astype(BF16)


def unpacked(sent):
    wide = sent.astype(F32)
    last = wide[TAPS : TAPS + 1] + wide[TAPS + 1 : TAPS + 2] + wide[TAPS + 2 : TAPS + 3]
    return jnp.concatenate([wide[:TAPS], last], axis=0)


def added(parts):
    sums = [unpacked(part) for part in parts]
    while len(sums) > 1:
        sums = [sums[at] + sums[at + 1] for at in range(0, len(sums), 2)]
    return sums[0]


def finish_kernel(*refs):
    parts, (d_conv, loss) = refs[:-2], refs[-2:]
    taps = [part[...].astype(F32)[0:TAPS] for part in parts]
    sums = []
    for part in parts:
        wide = part[...].astype(F32)
        sums.append(wide[TAPS : TAPS + 1] + wide[TAPS + 1 : TAPS + 2] + wide[TAPS + 2 : TAPS + 3])
    while len(taps) > 1:
        taps = [taps[at] + taps[at + 1] for at in range(0, len(taps), 2)]
        sums = [sums[at] + sums[at + 1] for at in range(0, len(sums), 2)]
    count = sums[0][:, 1:2]
    d_conv[...] = taps[0] / jnp.sqrt(count)
    loss[...] = sums[0][:, 0:1] / count


def call(kernel, operands, outs, scratch, places, flops, limit=24):
    specs = {
        "s": pl.BlockSpec(memory_space=pltpu.SMEM),
        "v": pl.BlockSpec(memory_space=pltpu.VMEM),
        "a": pl.BlockSpec(memory_space=pl.ANY),
    }
    arrays = list(operands) + list(outs)
    size = sum(math.prod(item.shape) * item.dtype.itemsize for item in arrays) if flops else 1
    return pl.pallas_call(
        kernel,
        out_shape=outs,
        in_specs=[specs[place] for place in places],
        out_specs=[specs["v"] for _ in outs],
        scratch_shapes=scratch,
        compiler_params=pltpu.CompilerParams(vmem_limit_bytes=limit * 1024 * 1024),
        cost_estimate=pl.CostEstimate(flops=max(flops, 1), bytes_accessed=size, transcendentals=0),
    )(*operands)


def local(
    queries,
    key_rows,
    value_rows,
    out_weight,
    head_weight,
    conv_weight,
    lengths,
    label_mask,
    targets,
):
    tokens, width = queries.shape[1:]
    depth = out_weight.shape[1]
    vocab = head_weight.shape[1]
    dp_size = lax.axis_size("dp")
    place = lax.axis_index("ctx")
    q, k, v = queries[0], key_rows[0], value_rows[0]
    info = jnp.stack([lengths[0], place * tokens, lax.axis_index("dp"), place % 2, (place // 2) % 2])
    info = info.astype(jnp.int32)

    shape = jax.ShapeDtypeStruct
    halo = shape((HALO, 2 * width), BF16)
    block = shape((tokens, width), BF16)
    half = head_weight.shape[0] // 2
    near, far, meta, piece = call(
        pack_kernel,
        (targets, label_mask, q, k, v, head_weight),
        (halo, halo, shape((tokens, 128), F32), shape((half, vocab), BF16)),
        [
            pltpu.VMEM((2, 2 * EDGE, width), BF16),
            pltpu.VMEM((2, 1, tokens), jnp.int32),
            pltpu.SemaphoreType.DMA((9,)),
        ],
        "aaaaaa",
        0,
        56,
    )
    q_own, k_own, v_own = call(stage_kernel, (q, k, v), (block, block, block), [], "vvv", 0)
    near, far = exchanged(near, far, "ctx")
    top_bit = bits_of(dp_size)[-1]
    far_piece = swapped(piece, "dp", top_bit)
    far_out = swapped(out_weight, "dp", top_bit)
    far_rest = swapped(far_piece, "ctx", 2)
    near, far, far_piece, far_out = lax.optimization_barrier((near, far, far_piece, far_out))
    ext = tokens + 2 * EDGE
    attn, lse, k_ext, v_ext, q_ext, meta_ext = call(
        attention_kernel,
        (info, q_own, k_own, v_own, meta, near, far),
        (
            shape((tokens + 32, width), BF16),
            shape((tokens, 128), F32),
            shape((tokens + 2 * HALO, width), BF16),
            shape((tokens + 2 * HALO, width), BF16),
            shape((tokens + 32, width), BF16),
            shape((ext, 128), F32),
        ),
        [],
        "svvvvvv",
        4 * tokens * 3 * WINDOW * width,
    )
    attn, far_rest = lax.optimization_barrier((attn, far_rest))
    spread = [
        [(0, 0, out_weight), (top_bit, 0, far_out)],
        [(0, 0, head_weight)],
        [(top_bit, 0, far_piece), (top_bit, 1, far_rest)],
    ]
    for bit in reversed(bits_of(dp_size)[:-1]):
        spread = [
            pieces + [(mark ^ bit, part, swapped(item, "dp", bit)) for mark, part, item in pieces]
            for pieces in spread
        ]
    marks = [[(mark, part) for mark, part, _ in pieces] for pieces in spread]
    held = [item for pieces in spread for _, _, item in pieces]

    chunks = depth // 128
    d_attn, stats, summary = call(
        functools.partial(middle_kernel, marks),
        (info, attn, lse, meta_ext, conv_weight, *held),
        (
            shape((tokens, width), BF16),
            shape((tokens, 128), F32),
            shape((16, depth), F32),
        ),
        [
            pltpu.VMEM((width, depth), BF16),
            pltpu.VMEM((depth, vocab), BF16),
            pltpu.VMEM((chunks, ext + 2 * EDGE, 128), F32),
            pltpu.VMEM((ext, depth), BF16),
            pltpu.VMEM((chunks, ext, 128), F32),
            pltpu.VMEM((ext, vocab), F32),
            pltpu.VMEM((ext, vocab), BF16),
            pltpu.VMEM((chunks, ext, 128), F32),
            pltpu.VMEM((tokens, depth), BF16),
            pltpu.SemaphoreType.DMA((len(held),)),
        ],
        "svvvv" + "a" * len(held),
        4 * tokens * depth * (width + vocab),
    )

    totals = summary[: TAPS + 1]
    dp_bits, ctx_bits = bits_of(dp_size), bits_of(lax.axis_size("ctx"))
    near_part, far_part = call(
        edge_grads_kernel,
        (info, q_ext, k_ext, v_ext, stats, d_attn),
        (shape((WINDOW, 2 * width), BF16), shape((WINDOW, 2 * width), BF16)),
        [],
        "svvvvv",
        16 * WINDOW * WINDOW * width,
    )
    steps = [("ctx", ctx_bits[:1])]
    steps += [("dp", group) for group in grouped(dp_bits)]
    steps += [("ctx", group) for group in grouped(ctx_bits[1:])]
    for index, (axis, group) in enumerate(steps):
        sent = packed(totals)
        got = [swapped(sent, axis, bit) for bit in group]
        if index == 0:
            near_part, far_part, d_attn, *got = lax.optimization_barrier(
                (near_part, far_part, d_attn, *got)
            )
            near_got, far_got = exchanged(near_part, far_part, "ctx")
        if index == len(steps) - 1:
            d_q, k_part, v_part = call(
                own_grads_kernel,
                (info, q_ext, k_ext, v_ext, stats, d_attn),
                (block, shape((tokens, width), F32), shape((tokens, width), F32)),
                [],
                "svvvvv",
                0,
            )
            d_q, k_part, v_part, *got = lax.optimization_barrier((d_q, k_part, v_part, *got))
        if index < len(steps) - 1:
            totals = added([sent] + got)
    d_k, d_v = call(
        add_kernel,
        (info, k_part, v_part, near_got, far_got),
        (block, block),
        [],
        "svvvv",
        tokens * width,
    )
    d_k, d_v, *got = lax.optimization_barrier((d_k, d_v, *got))
    d_conv, loss = call(
        finish_kernel,
        (sent, *got),
        (shape((TAPS, depth), F32), shape((1, 1), F32)),
        [],
        "v" * (1 + len(got)),
        0,
    )
    return (loss[0, 0], d_q[None], d_k[None], d_v[None], d_conv)


def solution(mesh):
    placed = (
        P("dp", "ctx", None),
        P("dp", "ctx", None),
        P("dp", "ctx", None),
        P("dp", None),
        P("dp", None),
        P(),
        P("dp"),
        P("dp", "ctx"),
        P("dp", "ctx"),
    )
    return jax.shard_map(
        local,
        mesh=mesh,
        in_specs=placed,
        out_specs=(P(), P("dp", "ctx", None), P("dp", "ctx", None), P("dp", "ctx", None), P()),
        check_vma=False,
    )
```

```python
import functools
import math

import jax
import jax.numpy as jnp
from jax import lax
from jax.experimental import pallas as pl
from jax.experimental.pallas import tpu as pltpu
from jax.sharding import PartitionSpec as P

HEAD_DIM = 128
WINDOW = 128
TAPS = 9
MARGIN = (TAPS - 1) // 2
EDGE = 8
HALO = WINDOW + 2 * EDGE
LOW = -1e30
FACTOR = 1.0 / math.sqrt(HEAD_DIM)
F32 = jnp.float32
BF16 = jnp.bfloat16


def bits_of(size):
    bits = []
    while (1 << len(bits)) < size:
        bits.append(1 << len(bits))
    return bits


def swapped(value, axis, bit):
    size = lax.axis_size(axis)
    return lax.ppermute(value, axis, [(i, i ^ bit) for i in range(size)])


def spread(pieces, axis):
    for bit in reversed(bits_of(lax.axis_size(axis))[:-1]):
        pieces = pieces + [(mark ^ bit, swapped(item, axis, bit)) for mark, item in pieces]
    return [mark for mark, _ in pieces], [item for _, item in pieces]


def exchanged(near, far, axis):
    size = lax.axis_size(axis)
    pairs = [(i, i ^ 1) for i in range(size) if (i ^ 1) < size]
    others = [(i, i - 1 + 2 * (i % 2)) for i in range(size) if 0 <= i - 1 + 2 * (i % 2) < size]
    return lax.ppermute(near, axis, pairs), lax.ppermute(far, axis, others)


def nt(left, right):
    return lax.dot_general(left, right, (((1,), (1,)), ((), ())), preferred_element_type=F32)


def tn(left, right):
    return lax.dot_general(left, right, (((0,), (0,)), ((), ())), preferred_element_type=F32)


def nn(left, right):
    return jnp.dot(left, right, preferred_element_type=F32)


def in_reach(query_pos, key_pos, offset, length):
    return (
        (jnp.abs(query_pos - key_pos) <= WINDOW)
        & (key_pos + offset >= 0)
        & (key_pos + offset < length)
    )


def pack_kernel(targets, mask, q, k, v, near, far, meta, edges, marks, sems):
    tokens, width = q.shape
    even = lax.rem(lax.axis_index("ctx"), 2) == 0
    edge = 2 * EDGE
    ends = (slice(0, edge), slice(tokens - edge, tokens))
    copies = []

    def fetch(source, target):
        copy = pltpu.make_async_copy(source, target, sems.at[len(copies)])
        copy.start()
        copies.append(copy)

    start = pl.multiple_of(jnp.where(even, tokens - HALO, 0), 16)
    other = pl.multiple_of(jnp.where(even, 0, tokens - HALO), 16)
    for message, first in ((near, start), (far, other)):
        fetch(k.at[pl.ds(first, HALO)], message.at[:, 0:width])
        fetch(v.at[pl.ds(first, HALO)], message.at[:, width : 2 * width])
    for place, end in enumerate(ends):
        fetch(q.at[end], edges.at[place])
    fetch(targets, marks.at[0])
    fetch(mask, marks.at[1])
    for copy in copies[-2:]:
        copy.wait()
    spread = (128, tokens)
    target = jnp.broadcast_to(marks[0], spread).T
    chosen = jnp.broadcast_to(marks[1], spread).T
    spot = lax.broadcasted_iota(jnp.int32, (tokens, 128), 1)
    entry = jnp.where(spot == 0, target >> 5, jnp.where(spot == 1, target & 31, chosen))
    meta[...] = entry.astype(F32)
    for copy in copies[:-2]:
        copy.wait()
    low = lax.broadcasted_iota(jnp.int32, (edge, 1), 0) < EDGE

    def patch(message, place, use, end):
        rows = slice(place, place + edge)
        held = message[rows, :].astype(F32)
        ours = jnp.concatenate(
            [edges[end].astype(F32), meta[ends[end], :], jnp.zeros((edge, width - 128), F32)],
            axis=1,
        )
        ours = jnp.concatenate([ours[EDGE:], ours[:EDGE]], axis=0)
        message[rows, :] = jnp.where(use, ours, held).astype(BF16)

    @pl.when(even)
    def _():
        patch(near, 0, low, 1)
        patch(far, HALO - edge, ~low, 0)

    @pl.when(~even)
    def _():
        patch(near, HALO - edge, ~low, 0)
        patch(far, 0, low, 1)


def stage_kernel(q, k, v, meta, q_own, k_own, v_own, meta_own):
    meta_own[...] = meta[...]
    q_own[...] = q[...]
    k_own[...] = k[...]
    v_own[...] = v[...]


def attention_kernel(
    info, q, k, v, meta, near, far, attn, lse, k_ext, v_ext, q_ext, meta_ext
):
    tokens, width = q.shape
    length, offset = info[0], info[1]
    even = info[3] == 0
    q_ext[16 : 16 + tokens, :] = q[...]
    k_ext[HALO : HALO + tokens, :] = k[...]
    v_ext[HALO : HALO + tokens, :] = v[...]

    def place_sides(left, right):
        for ext, first in ((k_ext, 0), (v_ext, width)):
            cols = slice(first, first + width)
            ext[0:HALO, :] = left[:, cols]
            ext[HALO + tokens : 2 * HALO + tokens, :] = right[:, cols]
        q_ext[0:16, :] = left[0:16, 0:width]
        q_ext[16 + tokens :, :] = right[HALO - 16 : HALO, 0:width]
        spots = slice(width, width + 128)
        meta_ext[0:EDGE, :] = left[0:16, spots].astype(F32)[0:EDGE]
        meta_ext[EDGE + tokens :, :] = right[HALO - 16 : HALO, spots].astype(F32)[EDGE:]

    @pl.when(even)
    def _():
        place_sides(far, near)

    @pl.when(~even)
    def _():
        place_sides(near, far)

    meta_ext[EDGE : EDGE + tokens, :] = meta[...]
    lse[...] = jnp.zeros(lse.shape, F32)
    rows, span = 16 + WINDOW, 4 * WINDOW
    spot = lax.broadcasted_iota(jnp.int32, (rows, span), 0)
    blocks = [
        (0, 0, jnp.where(spot < EDGE, spot - EDGE, spot - 16)),
        (
            tokens + 32 - rows,
            tokens + 2 * HALO - span,
            jnp.where(spot < WINDOW, spot + tokens - WINDOW, spot + tokens - WINDOW - EDGE),
        ),
    ]
    work = []
    for place, key_row, query_pos in blocks:
        key_pos = key_row - HALO + lax.broadcasted_iota(jnp.int32, (rows, span), 1)
        inside = in_reach(query_pos, key_pos, offset, length)
        keys = slice(key_row, key_row + span)
        work += [(place, keys, inside, at) for at in range(0, width, HEAD_DIM)]

    def scores_of(item):
        place, keys, inside, at = item
        cols = slice(at, at + HEAD_DIM)
        product = nt(q_ext[place : place + rows, cols], k_ext[keys, cols])
        return jnp.where(inside, product * FACTOR, LOW)

    scores = scores_of(work[0])
    for index, (place, keys, _, at) in enumerate(work):
        later = scores_of(work[index + 1]) if index + 1 < len(work) else None
        cols = slice(at, at + HEAD_DIM)
        head = at // HEAD_DIM
        top = jnp.max(scores, axis=-1, keepdims=True)
        grown = jnp.exp(scores - top)
        total = jnp.sum(grown, axis=-1, keepdims=True)
        mixed = nn(grown.astype(BF16), v_ext[keys, cols]) * (1.0 / total)
        attn[place : place + rows, cols] = mixed.astype(BF16)
        level = top + jnp.log(total)
        first = max(place, 16)
        lse[first - 16 : first - 16 + WINDOW, 4 + head : 5 + head] = level[
            first - place : first - place + WINDOW
        ]
        scores = later


def fetch_pieces(marks, mine, pieces, full, sems):
    copies = []
    for mark, piece in zip(marks, pieces):
        rows = piece.shape[0]
        target = full.at[pl.ds(pl.multiple_of((mine ^ mark) * rows, rows), rows)]
        copies.append(pltpu.make_async_copy(piece, target, sems.at[len(copies)]))
        copies[-1].start()
    return copies


def live_rows(info, rows, lanes):
    row_pos = info[1] - EDGE + lax.broadcasted_iota(jnp.int32, (rows, lanes), 0)
    return (row_pos >= 0) & (row_pos < info[0])


def hidden_kernel(marks, info, attn, *refs):
    pieces, (hid, out_full, sems) = refs[: len(marks)], refs[len(marks) :]
    copies = fetch_pieces(marks, info[2], pieces, out_full, sems)
    chunks, ext, lanes = hid.shape
    ext = ext - 2 * EDGE
    live = live_rows(info, ext, lanes)
    hid[:, 0:EDGE, :] = jnp.zeros((chunks, EDGE, lanes), F32)
    hid[:, EDGE + ext :, :] = jnp.zeros((chunks, EDGE, lanes), F32)
    for copy in copies:
        copy.wait()
    last = attn.shape[0] - 16
    for at in range(0, chunks * lanes, 256):
        block = nn(attn[...], out_full[:, at : at + 256])
        block = jnp.concatenate([block[0:EDGE], block[16:last], block[last + EDGE :]], axis=0)
        for part in range(2):
            piece = block[:, part * lanes : (part + 1) * lanes]
            hid[at // lanes + part, EDGE : EDGE + ext, :] = jnp.where(live, piece, 0.0)


def middle_kernel(marks, info, attn, lse, meta_ext, taps, hid, out_full, *refs):
    pieces, (d_attn, stats, summary) = refs[: len(marks)], refs[len(marks) : len(marks) + 3]
    head_full, gated, slope, logits, d_logits, d_pre, d_hid, sems = refs[len(marks) + 3 :]
    copies = fetch_pieces(marks, info[2], pieces, head_full, sems)
    tokens, width = d_attn.shape
    depth, vocab = head_full.shape
    ext = tokens + 2 * EDGE
    lanes = 128
    live = live_rows(info, ext, lanes)
    for chunk in range(depth // lanes):
        cols = slice(chunk * lanes, (chunk + 1) * lanes)
        conv = jnp.zeros((ext, lanes), F32)
        for tap in range(TAPS):
            start = EDGE - MARGIN + tap
            conv = conv + taps[tap : tap + 1, cols] * hid[chunk, start : start + ext, :]
        sigma = jax.nn.sigmoid(conv)
        gated[:, cols] = (conv * sigma).astype(BF16)
        slope[chunk] = sigma * (1.0 + conv * (1.0 - sigma))
    for copy in copies:
        copy.wait()
    for at in range(0, vocab, 256):
        logits[:, at : at + 256] = nn(gated[...], head_full[:, at : at + 256])

    meta_all = meta_ext[...]
    target = (meta_all[:, 0:1] * 32.0 + meta_all[:, 1:2]).astype(jnp.int32)
    chosen = jnp.where(live & (meta_all[:, 2:3] == 1.0), 1.0, 0.0)[:, 0:1]
    loss_rows = jnp.zeros((16, 1), F32)
    count_rows = jnp.zeros((16, 1), F32)
    word = lax.broadcasted_iota(jnp.int32, (16, vocab), 1)
    row_in = lax.broadcasted_iota(jnp.int32, (16, 1), 0)
    for at in range(0, ext, 16):
        block = logits[at : at + 16, :]
        top = jnp.max(block, axis=-1, keepdims=True)
        grown = jnp.exp(block - top)
        total = jnp.sum(grown, axis=-1, keepdims=True)
        hit = target[at : at + 16] == word
        picked = jnp.sum(jnp.where(hit, block, 0.0), axis=-1, keepdims=True)
        pick = chosen[at : at + 16]
        change = grown * (pick / total) - jnp.where(hit, pick, 0.0)
        d_logits[at : at + 16, :] = change.astype(BF16)
        own = (row_in + at >= EDGE) & (row_in + at < EDGE + tokens)
        kept = jnp.where(own, pick, 0.0)
        loss_rows = loss_rows + kept * (top + jnp.log(total) - picked)
        count_rows = count_rows + kept
    summary[...] = jnp.zeros(summary.shape, F32)
    lane = lax.broadcasted_iota(jnp.int32, (1, lanes), 1)
    loss_sum = jnp.sum(loss_rows, axis=0, keepdims=True)
    count_sum = jnp.sum(count_rows, axis=0, keepdims=True)
    summary[TAPS : TAPS + 1, 0:lanes] = jnp.where(
        lane == 0, loss_sum, jnp.where(lane == 1, count_sum, 0.0)
    )
    for at in range(0, depth, 256):
        d_gated = nt(d_logits[...], head_full[at : at + 256, :])
        for part in range(2):
            chunk = at // lanes + part
            cols = slice(chunk * lanes, (chunk + 1) * lanes)
            change = d_gated[:, part * lanes : (part + 1) * lanes] * slope[chunk]
            d_pre[chunk] = change
            owned = change[EDGE : EDGE + tokens]
            for tap in range(TAPS):
                start = 2 * EDGE - MARGIN + tap
                summary[tap : tap + 1, cols] = jnp.sum(
                    owned * hid[chunk, start : start + tokens, :], axis=0, keepdims=True
                )
    for chunk in range(depth // lanes):
        cols = slice(chunk * lanes, (chunk + 1) * lanes)
        change = jnp.zeros((tokens, lanes), F32)
        for tap in range(TAPS):
            start = EDGE + MARGIN - tap
            change = change + taps[tap : tap + 1, cols] * d_pre[chunk, start : start + tokens, :]
        d_hid[:, cols] = jnp.where(live[EDGE : EDGE + tokens], change, 0.0).astype(BF16)
    stats[...] = lse[...]
    for at in range(0, width, HEAD_DIM):
        cols = slice(at, at + HEAD_DIM)
        head = at // HEAD_DIM
        block = nt(d_hid[...], out_full[cols, :]).astype(BF16)
        d_attn[:, cols] = block
        products = block.astype(F32) * attn[16 : 16 + tokens, cols].astype(F32)
        stats[:, head : head + 1] = jnp.sum(products, axis=-1, keepdims=True)


def edge_grads_kernel(info, q_ext, k_ext, v_ext, stats, d_attn, near, far):
    tokens, width = d_attn.shape
    length, offset = info[0], info[1]
    even = info[3] == 0
    work = []
    for out, on_right in ((near, even), (far, ~even)):
        first = pl.multiple_of(jnp.where(on_right, tokens - WINDOW, 0), WINDOW)
        key_start = jnp.where(on_right, tokens, -WINDOW)
        rows = pl.ds(first, WINDOW)
        asked = pl.ds(pl.multiple_of(first + 16, 16), WINDOW)
        keys = pl.ds(pl.multiple_of(key_start + HALO, 16), WINDOW)
        by_row = stats[rows, :].T
        key_pos = key_start + lax.broadcasted_iota(jnp.int32, (WINDOW, WINDOW), 0)
        query_pos = first + lax.broadcasted_iota(jnp.int32, (WINDOW, WINDOW), 1)
        inside = in_reach(query_pos, key_pos, offset, length)
        for head in range(width // HEAD_DIM):
            cols = slice(head * HEAD_DIM, (head + 1) * HEAD_DIM)
            query, change = q_ext[asked, cols], d_attn[rows, cols]
            scores = jnp.where(inside, nt(k_ext[keys, cols], query) * FACTOR, LOW)
            d_probs = nt(v_ext[keys, cols], change)
            work.append((out, head, by_row, query, change, scores, d_probs))
    done = []
    for out, head, by_row, query, change, scores, d_probs in work:
        probs = jnp.exp(scores - by_row[4 + head : 5 + head, :])
        d_scores = probs * (d_probs - by_row[head : head + 1, :])
        done.append((out, head, query, change, d_scores.astype(BF16), probs.astype(BF16)))
    for out, head, query, change, d_scores, probs in done:
        cols = slice(head * HEAD_DIM, (head + 1) * HEAD_DIM)
        out[:, cols] = (nn(d_scores, query) * FACTOR).astype(BF16)
        cols = slice(width + head * HEAD_DIM, width + (head + 1) * HEAD_DIM)
        out[:, cols] = nn(probs, change).astype(BF16)


def own_grads_kernel(info, q_ext, k_ext, v_ext, stats, d_attn, d_q, d_k, d_v):
    tokens, width = d_attn.shape
    length, offset = info[0], info[1]
    span = tokens + 2 * WINDOW
    keys = slice(HALO - WINDOW, HALO + tokens + WINDOW)
    own = slice(WINDOW, WINDOW + tokens)
    by_row = stats[...].T
    key_pos = lax.broadcasted_iota(jnp.int32, (span, tokens), 0) - WINDOW
    query_pos = lax.broadcasted_iota(jnp.int32, (span, tokens), 1)
    inside = in_reach(query_pos, key_pos, offset, length)

    def products_of(head):
        cols = slice(head * HEAD_DIM, (head + 1) * HEAD_DIM)
        scores = nt(k_ext[keys, cols], q_ext[16 : 16 + tokens, cols])
        return jnp.where(inside, scores * FACTOR, LOW), nt(v_ext[keys, cols], d_attn[:, cols])

    heads = width // HEAD_DIM
    products = products_of(0)
    for head in range(heads):
        later = products_of(head + 1) if head + 1 < heads else None
        cols = slice(head * HEAD_DIM, (head + 1) * HEAD_DIM)
        scores, d_probs = products
        probs = jnp.exp(scores - by_row[4 + head : 5 + head, :])
        d_scores = (probs * (d_probs - by_row[head : head + 1, :])).astype(BF16)
        d_k[:, cols] = nn(d_scores[own], q_ext[16 : 16 + tokens, cols]) * FACTOR
        d_v[:, cols] = nn(probs[own].astype(BF16), d_attn[:, cols])
        d_q[:, cols] = (tn(k_ext[keys, cols], d_scores) * FACTOR).T.astype(BF16)
        products = later


def grouped(bits):
    pairs = [bits[at : at + 2] for at in range(0, len(bits), 2)]
    return [pair + [pair[0] ^ pair[1]] if len(pair) == 2 else pair for pair in pairs]


def packed(totals):
    rounded = lax.reduce_precision(totals[:TAPS], 8, 7)
    first = lax.reduce_precision(totals[TAPS:], 8, 7)
    second = lax.reduce_precision(totals[TAPS:] - first, 8, 7)
    third = totals[TAPS:] - first - second
    return jnp.concatenate([rounded, first, second, third], axis=0).astype(BF16)


def unpacked(sent):
    wide = sent.astype(F32)
    last = wide[TAPS : TAPS + 1] + wide[TAPS + 1 : TAPS + 2] + wide[TAPS + 2 : TAPS + 3]
    return jnp.concatenate([wide[:TAPS], last], axis=0)


def added(parts):
    sums = [unpacked(part) for part in parts]
    while len(sums) > 1:
        sums = [sums[at] + sums[at + 1] for at in range(0, len(sums), 2)]
    return sums[0]


def finish_kernel(info, k_part, v_part, near, far, *refs):
    parts, (d_k, d_v, d_conv, loss) = refs[:-4], refs[-4:]
    tokens, width = d_k.shape
    even = info[3] == 0
    for got, on_right in ((near, even), (far, ~even)):
        rows = pl.ds(pl.multiple_of(jnp.where(on_right, tokens - WINDOW, 0), WINDOW), WINDOW)
        for out, part, cols in (
            (d_k, k_part, slice(0, width)),
            (d_v, v_part, slice(width, 2 * width)),
        ):
            out[rows, :] = (part[rows, :] + got[:, cols].astype(F32)).astype(BF16)
    taps = [part[...].astype(F32)[0:TAPS] for part in parts]
    sums = []
    for part in parts:
        wide = part[...].astype(F32)
        sums.append(wide[TAPS : TAPS + 1] + wide[TAPS + 1 : TAPS + 2] + wide[TAPS + 2 : TAPS + 3])
    while len(taps) > 1:
        taps = [taps[at] + taps[at + 1] for at in range(0, len(taps), 2)]
        sums = [sums[at] + sums[at + 1] for at in range(0, len(sums), 2)]
    count = sums[0][:, 1:2]
    d_conv[...] = taps[0] / jnp.sqrt(count)
    loss[...] = sums[0][:, 0:1] / count


def call(kernel, operands, outs, scratch, places, flops, limit=24):
    specs = {
        "s": pl.BlockSpec(memory_space=pltpu.SMEM),
        "v": pl.BlockSpec(memory_space=pltpu.VMEM),
        "a": pl.BlockSpec(memory_space=pl.ANY),
    }
    arrays = list(operands) + list(outs)
    size = sum(math.prod(item.shape) * item.dtype.itemsize for item in arrays) if flops else 1
    return pl.pallas_call(
        kernel,
        out_shape=outs,
        in_specs=[specs[place] for place in places],
        out_specs=[specs["v"] for _ in outs],
        scratch_shapes=scratch,
        compiler_params=pltpu.CompilerParams(vmem_limit_bytes=limit * 1024 * 1024),
        cost_estimate=pl.CostEstimate(flops=max(flops, 1), bytes_accessed=size, transcendentals=0),
    )(*operands)


def local(
    queries,
    key_rows,
    value_rows,
    out_weight,
    head_weight,
    conv_weight,
    lengths,
    label_mask,
    targets,
):
    tokens, width = queries.shape[1:]
    depth = out_weight.shape[1]
    vocab = head_weight.shape[1]
    dp_size = lax.axis_size("dp")
    place = lax.axis_index("ctx")
    q, k, v = queries[0], key_rows[0], value_rows[0]
    info = jnp.stack([lengths[0], place * tokens, lax.axis_index("dp"), place % 2])
    info = info.astype(jnp.int32)

    shape = jax.ShapeDtypeStruct
    halo = shape((HALO, 2 * width), BF16)
    block = shape((tokens, width), BF16)
    near, far, meta = call(
        pack_kernel,
        (targets, label_mask, q, k, v),
        (halo, halo, shape((tokens, 128), F32)),
        [
            pltpu.VMEM((2, 2 * EDGE, width), BF16),
            pltpu.VMEM((2, 1, tokens), jnp.int32),
            pltpu.SemaphoreType.DMA((8,)),
        ],
        "aaaaa",
        0,
        56,
    )
    q_own, k_own, v_own, meta = call(
        stage_kernel,
        (q, k, v, meta),
        (block, block, block, shape((tokens, 128), F32)),
        [],
        "vvvv",
        0,
    )
    near, far, head_weight = lax.optimization_barrier((near, far, head_weight))
    near, far = exchanged(near, far, "ctx")
    top_bit = bits_of(dp_size)[-1]
    far_out = swapped(out_weight, "dp", top_bit)
    far_head = swapped(head_weight, "dp", top_bit)
    out_marks, out_held = spread([(0, out_weight), (top_bit, far_out)], "dp")
    near, far, *out_held = lax.optimization_barrier((near, far, *out_held))

    ext = tokens + 2 * EDGE
    attn, lse, k_ext, v_ext, q_ext, meta_ext = call(
        attention_kernel,
        (info, q_own, k_own, v_own, meta, near, far),
        (
            shape((tokens + 32, width), BF16),
            shape((tokens, 128), F32),
            shape((tokens + 2 * HALO, width), BF16),
            shape((tokens + 2 * HALO, width), BF16),
            shape((tokens + 32, width), BF16),
            shape((ext, 128), F32),
        ),
        [],
        "svvvvvv",
        4 * tokens * 3 * WINDOW * width,
    )
    attn, far_head = lax.optimization_barrier((attn, far_head))
    head_marks, head_held = spread([(0, head_weight), (top_bit, far_head)], "dp")

    chunks = depth // 128
    hid, out_full = call(
        functools.partial(hidden_kernel, out_marks),
        (info, attn, *out_held),
        (shape((chunks, ext + 2 * EDGE, 128), F32), shape((width, depth), BF16)),
        [pltpu.SemaphoreType.DMA((len(out_held),))],
        "sv" + "a" * len(out_held),
        2 * tokens * depth * width,
    )
    d_attn, stats, summary = call(
        functools.partial(middle_kernel, head_marks),
        (info, attn, lse, meta_ext, conv_weight, hid, out_full, *head_held),
        (
            shape((tokens, width), BF16),
            shape((tokens, 128), F32),
            shape((16, depth), F32),
        ),
        [
            pltpu.VMEM((depth, vocab), BF16),
            pltpu.VMEM((ext, depth), BF16),
            pltpu.VMEM((chunks, ext, 128), F32),
            pltpu.VMEM((ext, vocab), F32),
            pltpu.VMEM((ext, vocab), BF16),
            pltpu.VMEM((chunks, ext, 128), F32),
            pltpu.VMEM((tokens, depth), BF16),
            pltpu.SemaphoreType.DMA((len(head_held),)),
        ],
        "svvvvvv" + "a" * len(head_held),
        4 * tokens * depth * (width + vocab),
    )

    totals = summary[: TAPS + 1]
    dp_bits, ctx_bits = bits_of(dp_size), bits_of(lax.axis_size("ctx"))
    near_part, far_part = call(
        edge_grads_kernel,
        (info, q_ext, k_ext, v_ext, stats, d_attn),
        (shape((WINDOW, 2 * width), BF16), shape((WINDOW, 2 * width), BF16)),
        [],
        "svvvvv",
        16 * WINDOW * WINDOW * width,
    )
    steps = [("ctx", ctx_bits[:1])]
    steps += [("dp", group) for group in grouped(dp_bits)]
    steps += [("ctx", group) for group in grouped(ctx_bits[1:])]
    for index, (axis, group) in enumerate(steps):
        sent = packed(totals)
        got = [swapped(sent, axis, bit) for bit in group]
        if index == 0:
            near_part, far_part, d_attn, *got = lax.optimization_barrier(
                (near_part, far_part, d_attn, *got)
            )
            near_got, far_got = exchanged(near_part, far_part, "ctx")
        if index == len(steps) - 1:
            d_q, k_part, v_part = call(
                own_grads_kernel,
                (info, q_ext, k_ext, v_ext, stats, d_attn),
                (block, shape((tokens, width), F32), shape((tokens, width), F32)),
                [],
                "svvvvv",
                0,
            )
            d_q, k_part, v_part, *got = lax.optimization_barrier((d_q, k_part, v_part, *got))
        if index < len(steps) - 1:
            totals = added([sent] + got)
    d_k, d_v, d_conv, loss = call(
        finish_kernel,
        (info, k_part, v_part, near_got, far_got, sent, *got),
        (block, block, shape((TAPS, depth), F32), shape((1, 1), F32)),
        [],
        "svvvv" + "v" * (1 + len(got)),
        tokens * width,
    )
    return (loss[0, 0], d_q[None], d_k[None], d_v[None], d_conv)


def solution(mesh):
    placed = (
        P("dp", "ctx", None),
        P("dp", "ctx", None),
        P("dp", "ctx", None),
        P("dp", None),
        P("dp", None),
        P(),
        P("dp"),
        P("dp", "ctx"),
        P("dp", "ctx"),
    )
    return jax.shard_map(
        local,
        mesh=mesh,
        in_specs=placed,
        out_specs=(P(), P("dp", "ctx", None), P("dp", "ctx", None), P("dp", "ctx", None), P()),
        check_vma=False,
    )
```

```python
import functools
import math

import jax
import jax.numpy as jnp
from jax import lax
from jax.experimental import pallas as pl
from jax.experimental.pallas import tpu as pltpu
from jax.sharding import PartitionSpec as P

HEAD_DIM = 128
WINDOW = 128
TAPS = 9
MARGIN = (TAPS - 1) // 2
EDGE = 8
HALO = WINDOW + 2 * EDGE
LOW = -1e30
FACTOR = 1.0 / math.sqrt(HEAD_DIM)
F32 = jnp.float32
BF16 = jnp.bfloat16


def bits_of(size):
    bits = []
    while (1 << len(bits)) < size:
        bits.append(1 << len(bits))
    return bits


def swapped(value, axis, bit):
    size = lax.axis_size(axis)
    return lax.ppermute(value, axis, [(i, i ^ bit) for i in range(size)])


def spread(pieces, axis):
    for bit in reversed(bits_of(lax.axis_size(axis))[:-1]):
        pieces = pieces + [(mark ^ bit, swapped(item, axis, bit)) for mark, item in pieces]
    return [mark for mark, _ in pieces], [item for _, item in pieces]


def exchanged(near, far, axis):
    size = lax.axis_size(axis)
    pairs = [(i, i ^ 1) for i in range(size) if (i ^ 1) < size]
    others = [(i, i - 1 + 2 * (i % 2)) for i in range(size) if 0 <= i - 1 + 2 * (i % 2) < size]
    return lax.ppermute(near, axis, pairs), lax.ppermute(far, axis, others)


def nt(left, right):
    return lax.dot_general(left, right, (((1,), (1,)), ((), ())), preferred_element_type=F32)


def tn(left, right):
    return lax.dot_general(left, right, (((0,), (0,)), ((), ())), preferred_element_type=F32)


def nn(left, right):
    return jnp.dot(left, right, preferred_element_type=F32)


def in_reach(query_pos, key_pos, offset, length):
    return (
        (jnp.abs(query_pos - key_pos) <= WINDOW)
        & (key_pos + offset >= 0)
        & (key_pos + offset < length)
    )


def pack_kernel(targets, mask, q, k, v, near, far, meta, edges, marks, sems):
    tokens, width = q.shape
    even = lax.rem(lax.axis_index("ctx"), 2) == 0
    edge = 2 * EDGE
    ends = (slice(0, edge), slice(tokens - edge, tokens))
    copies = []

    def fetch(source, target):
        copy = pltpu.make_async_copy(source, target, sems.at[len(copies)])
        copy.start()
        copies.append(copy)

    start = pl.multiple_of(jnp.where(even, tokens - HALO, 0), 16)
    other = pl.multiple_of(jnp.where(even, 0, tokens - HALO), 16)
    for message, first in ((near, start), (far, other)):
        fetch(k.at[pl.ds(first, HALO)], message.at[:, 0:width])
        fetch(v.at[pl.ds(first, HALO)], message.at[:, width : 2 * width])
    for place, end in enumerate(ends):
        fetch(q.at[end], edges.at[place])
    fetch(targets, marks.at[0])
    fetch(mask, marks.at[1])
    for copy in copies[-2:]:
        copy.wait()
    spread = (128, tokens)
    target = jnp.broadcast_to(marks[0], spread).T
    chosen = jnp.broadcast_to(marks[1], spread).T
    spot = lax.broadcasted_iota(jnp.int32, (tokens, 128), 1)
    entry = jnp.where(spot == 0, target >> 5, jnp.where(spot == 1, target & 31, chosen))
    meta[...] = entry.astype(F32)
    for copy in copies[:-2]:
        copy.wait()
    low = lax.broadcasted_iota(jnp.int32, (edge, 1), 0) < EDGE

    def patch(message, place, use, end):
        rows = slice(place, place + edge)
        held = message[rows, :].astype(F32)
        ours = jnp.concatenate(
            [edges[end].astype(F32), meta[ends[end], :], jnp.zeros((edge, width - 128), F32)],
            axis=1,
        )
        ours = jnp.concatenate([ours[EDGE:], ours[:EDGE]], axis=0)
        message[rows, :] = jnp.where(use, ours, held).astype(BF16)

    @pl.when(even)
    def _():
        patch(near, 0, low, 1)
        patch(far, HALO - edge, ~low, 0)

    @pl.when(~even)
    def _():
        patch(near, HALO - edge, ~low, 0)
        patch(far, 0, low, 1)


def stage_kernel(q, k, v, q_own, k_own, v_own):
    q_own[...] = q[...]
    k_own[...] = k[...]
    v_own[...] = v[...]


def attention_kernel(
    info, q, k, v, near, far, attn, lse, k_ext, v_ext, q_ext, meta_edges
):
    tokens, width = q.shape
    length, offset = info[0], info[1]
    even = info[3] == 0
    q_ext[16 : 16 + tokens, :] = q[...]
    k_ext[HALO : HALO + tokens, :] = k[...]
    v_ext[HALO : HALO + tokens, :] = v[...]

    def place_sides(left, right):
        for ext, first in ((k_ext, 0), (v_ext, width)):
            cols = slice(first, first + width)
            ext[0:HALO, :] = left[:, cols]
            ext[HALO + tokens : 2 * HALO + tokens, :] = right[:, cols]
        q_ext[0:16, :] = left[0:16, 0:width]
        q_ext[16 + tokens :, :] = right[HALO - 16 : HALO, 0:width]
        spots = slice(width, width + 128)
        meta_edges[0:EDGE, :] = left[0:16, spots].astype(F32)[0:EDGE]
        meta_edges[EDGE:, :] = right[HALO - 16 : HALO, spots].astype(F32)[EDGE:]

    @pl.when(even)
    def _():
        place_sides(far, near)

    @pl.when(~even)
    def _():
        place_sides(near, far)

    lse[...] = jnp.zeros(lse.shape, F32)
    rows, span = 16 + WINDOW, 4 * WINDOW
    spot = lax.broadcasted_iota(jnp.int32, (rows, span), 0)
    blocks = [
        (0, 0, jnp.where(spot < EDGE, spot - EDGE, spot - 16)),
        (
            tokens + 32 - rows,
            tokens + 2 * HALO - span,
            jnp.where(spot < WINDOW, spot + tokens - WINDOW, spot + tokens - WINDOW - EDGE),
        ),
    ]
    work = []
    for place, key_row, query_pos in blocks:
        key_pos = key_row - HALO + lax.broadcasted_iota(jnp.int32, (rows, span), 1)
        inside = in_reach(query_pos, key_pos, offset, length)
        keys = slice(key_row, key_row + span)
        work += [(place, keys, inside, at) for at in range(0, width, HEAD_DIM)]

    def scores_of(item):
        place, keys, inside, at = item
        cols = slice(at, at + HEAD_DIM)
        product = nt(q_ext[place : place + rows, cols], k_ext[keys, cols])
        return jnp.where(inside, product * FACTOR, LOW)

    scores = scores_of(work[0])
    for index, (place, keys, _, at) in enumerate(work):
        later = scores_of(work[index + 1]) if index + 1 < len(work) else None
        cols = slice(at, at + HEAD_DIM)
        head = at // HEAD_DIM
        top = jnp.max(scores, axis=-1, keepdims=True)
        grown = jnp.exp(scores - top)
        total = jnp.sum(grown, axis=-1, keepdims=True)
        mixed = nn(grown.astype(BF16), v_ext[keys, cols]) * (1.0 / total)
        attn[place : place + rows, cols] = mixed.astype(BF16)
        level = top + jnp.log(total)
        first = max(place, 16)
        lse[first - 16 : first - 16 + WINDOW, 4 + head : 5 + head] = level[
            first - place : first - place + WINDOW
        ]
        scores = later


def fetch_pieces(marks, mine, pieces, full, sems, first=0):
    copies = []
    held = full.shape[0] // pieces[0].shape[0]
    for mark, piece in zip(marks, pieces):
        rows = piece.shape[0]
        start = ((mine ^ mark) & (held - 1)) * rows
        target = full.at[pl.ds(pl.multiple_of(start, rows), rows)]
        copies.append(pltpu.make_async_copy(piece, target, sems.at[first + len(copies)]))
        copies[-1].start()
    return copies


def live_rows(info, rows, lanes):
    row_pos = info[1] - EDGE + lax.broadcasted_iota(jnp.int32, (rows, lanes), 0)
    return (row_pos >= 0) & (row_pos < info[0])


def hidden_kernel(marks, info, attn, taps, *refs):
    pieces, (hid, out_full, gated, slope, sems) = refs[: len(marks)], refs[len(marks) :]
    copies = fetch_pieces(marks, info[2], pieces, out_full, sems)
    chunks, ext, lanes = hid.shape
    depth = chunks * lanes
    ext = ext - 2 * EDGE
    live = live_rows(info, ext, lanes)
    hid[:, 0:EDGE, :] = jnp.zeros((chunks, EDGE, lanes), F32)
    hid[:, EDGE + ext :, :] = jnp.zeros((chunks, EDGE, lanes), F32)
    for copy in copies:
        copy.wait()
    last = attn.shape[0] - 16
    for at in range(0, chunks * lanes, 256):
        block = nn(attn[...], out_full[:, at : at + 256])
        block = jnp.concatenate([block[0:EDGE], block[16:last], block[last + EDGE :]], axis=0)
        for part in range(2):
            piece = block[:, part * lanes : (part + 1) * lanes]
            hid[at // lanes + part, EDGE : EDGE + ext, :] = jnp.where(live, piece, 0.0)
    for chunk in range(depth // lanes):
        cols = slice(chunk * lanes, (chunk + 1) * lanes)
        conv = jnp.zeros((ext, lanes), F32)
        for tap in range(TAPS):
            start = EDGE - MARGIN + tap
            conv = conv + taps[tap : tap + 1, cols] * hid[chunk, start : start + ext, :]
        sigma = jax.nn.sigmoid(conv)
        gated[:, cols] = (conv * sigma).astype(BF16)
        slope[chunk] = sigma * (1.0 + conv * (1.0 - sigma))


def middle_kernel(
    marks, info, attn, lse, meta, meta_edges, taps, hid, out_full, gated, slope, *refs
):
    pieces, (d_attn, stats, summary) = refs[: len(marks)], refs[len(marks) : len(marks) + 3]
    head_own, head_far, logits, d_logits, d_pre, d_hid, sems = refs[len(marks) + 3 :]
    count = len(marks) // 2
    others = fetch_pieces(marks[:count], info[2], pieces[:count], head_own, sems)
    copies = fetch_pieces(marks[count:], info[2], pieces[count:], head_far, sems, count)
    tokens, width = d_attn.shape
    half, vocab = head_far.shape
    depth = 2 * half
    on_top = (info[2] & count) != 0
    own_start = pl.multiple_of(jnp.where(on_top, half, 0), half)
    far_start = pl.multiple_of(jnp.where(on_top, 0, half), half)
    ext = tokens + 2 * EDGE
    lanes = 128
    live = live_rows(info, ext, lanes)
    for copy in others:
        copy.wait()
    for at in range(0, vocab, 256):
        cols = slice(at, at + 256)
        logits[:, cols] = nn(gated[:, pl.ds(own_start, half)], head_own[:, cols])
    for copy in copies:
        copy.wait()
    for at in range(0, vocab, 256):
        cols = slice(at, at + 256)
        logits[:, cols] += nn(gated[:, pl.ds(far_start, half)], head_far[:, cols])
    meta_all = jnp.concatenate([meta_edges[0:EDGE], meta[...], meta_edges[EDGE:]], axis=0)
    target = (meta_all[:, 0:1] * 32.0 + meta_all[:, 1:2]).astype(jnp.int32)
    chosen = jnp.where(live & (meta_all[:, 2:3] == 1.0), 1.0, 0.0)[:, 0:1]
    loss_rows = jnp.zeros((16, 1), F32)
    count_rows = jnp.zeros((16, 1), F32)
    word = lax.broadcasted_iota(jnp.int32, (16, vocab), 1)
    row_in = lax.broadcasted_iota(jnp.int32, (16, 1), 0)
    for at in range(0, ext, 16):
        block = logits[at : at + 16, :]
        top = jnp.max(block, axis=-1, keepdims=True)
        grown = jnp.exp(block - top)
        total = jnp.sum(grown, axis=-1, keepdims=True)
        hit = target[at : at + 16] == word
        picked = jnp.sum(jnp.where(hit, block, 0.0), axis=-1, keepdims=True)
        pick = chosen[at : at + 16]
        change = grown * (pick / total) - jnp.where(hit, pick, 0.0)
        d_logits[at : at + 16, :] = change.astype(BF16)
        own = (row_in + at >= EDGE) & (row_in + at < EDGE + tokens)
        kept = jnp.where(own, pick, 0.0)
        loss_rows = loss_rows + kept * (top + jnp.log(total) - picked)
        count_rows = count_rows + kept
    summary[...] = jnp.zeros(summary.shape, F32)
    lane = lax.broadcasted_iota(jnp.int32, (1, lanes), 1)
    loss_sum = jnp.sum(loss_rows, axis=0, keepdims=True)
    count_sum = jnp.sum(count_rows, axis=0, keepdims=True)
    summary[TAPS : TAPS + 1, 0:lanes] = jnp.where(
        lane == 0, loss_sum, jnp.where(lane == 1, count_sum, 0.0)
    )
    turns = [
        (held, start, at)
        for held, start in ((head_own, own_start), (head_far, far_start))
        for at in range(0, half, 256)
    ]
    d_gated = nt(d_logits[...], head_own[0:256, :])
    for turn, (_, start, at) in enumerate(turns):
        later = None
        if turn + 1 < len(turns):
            held, _, following = turns[turn + 1]
            later = nt(d_logits[...], held[following : following + 256, :])
        for part in range(2):
            chunk = start // lanes + at // lanes + part
            cols = pl.ds(pl.multiple_of(start + at + part * lanes, lanes), lanes)
            change = d_gated[:, part * lanes : (part + 1) * lanes] * slope[chunk]
            d_pre[chunk] = change
            owned = change[EDGE : EDGE + tokens]
            for tap in range(TAPS):
                row = 2 * EDGE - MARGIN + tap
                summary[tap : tap + 1, cols] = jnp.sum(
                    owned * hid[chunk, row : row + tokens, :], axis=0, keepdims=True
                )
        d_gated = later
    for chunk in range(depth // lanes):
        cols = slice(chunk * lanes, (chunk + 1) * lanes)
        change = jnp.zeros((tokens, lanes), F32)
        for tap in range(TAPS):
            start = EDGE + MARGIN - tap
            change = change + taps[tap : tap + 1, cols] * d_pre[chunk, start : start + tokens, :]
        d_hid[:, cols] = jnp.where(live[EDGE : EDGE + tokens], change, 0.0).astype(BF16)
    stats[...] = lse[...]
    blocks = [
        nt(d_hid[...], out_full[at : at + 2 * HEAD_DIM, :]).astype(BF16)
        for at in range(0, width, 2 * HEAD_DIM)
    ]
    for place, pair in enumerate(blocks):
        for part in range(2):
            head = 2 * place + part
            cols = slice(head * HEAD_DIM, (head + 1) * HEAD_DIM)
            block = pair[:, part * HEAD_DIM : (part + 1) * HEAD_DIM]
            d_attn[:, cols] = block
            products = block.astype(F32) * attn[16 : 16 + tokens, cols].astype(F32)
            stats[:, head : head + 1] = jnp.sum(products, axis=-1, keepdims=True)


def edge_grads_kernel(info, q_ext, k_ext, v_ext, stats, d_attn, near, far):
    tokens, width = d_attn.shape
    length, offset = info[0], info[1]
    even = info[3] == 0
    work = []
    for out, on_right in ((near, even), (far, ~even)):
        first = pl.multiple_of(jnp.where(on_right, tokens - WINDOW, 0), WINDOW)
        key_start = jnp.where(on_right, tokens, -WINDOW)
        rows = pl.ds(first, WINDOW)
        asked = pl.ds(pl.multiple_of(first + 16, 16), WINDOW)
        keys = pl.ds(pl.multiple_of(key_start + HALO, 16), WINDOW)
        by_row = stats[rows, :].T
        key_pos = key_start + lax.broadcasted_iota(jnp.int32, (WINDOW, WINDOW), 0)
        query_pos = first + lax.broadcasted_iota(jnp.int32, (WINDOW, WINDOW), 1)
        inside = in_reach(query_pos, key_pos, offset, length)
        for head in range(width // HEAD_DIM):
            cols = slice(head * HEAD_DIM, (head + 1) * HEAD_DIM)
            query, change = q_ext[asked, cols], d_attn[rows, cols]
            scores = jnp.where(inside, nt(k_ext[keys, cols], query) * FACTOR, LOW)
            d_probs = nt(v_ext[keys, cols], change)
            work.append((out, head, by_row, query, change, scores, d_probs))
    done = []
    for out, head, by_row, query, change, scores, d_probs in work:
        probs = jnp.exp(scores - by_row[4 + head : 5 + head, :])
        d_scores = probs * (d_probs - by_row[head : head + 1, :])
        done.append((out, head, query, change, d_scores.astype(BF16), probs.astype(BF16)))
    for out, head, query, change, d_scores, probs in done:
        cols = slice(head * HEAD_DIM, (head + 1) * HEAD_DIM)
        out[:, cols] = (nn(d_scores, query) * FACTOR).astype(BF16)
        cols = slice(width + head * HEAD_DIM, width + (head + 1) * HEAD_DIM)
        out[:, cols] = nn(probs, change).astype(BF16)


def own_grads_kernel(info, q_ext, k_ext, v_ext, stats, d_attn, d_q, d_k, d_v):
    tokens, width = d_attn.shape
    length, offset = info[0], info[1]
    span = tokens + 2 * WINDOW
    keys = slice(HALO - WINDOW, HALO + tokens + WINDOW)
    own = slice(WINDOW, WINDOW + tokens)
    by_row = stats[...].T
    key_pos = lax.broadcasted_iota(jnp.int32, (span, tokens), 0) - WINDOW
    query_pos = lax.broadcasted_iota(jnp.int32, (span, tokens), 1)
    inside = in_reach(query_pos, key_pos, offset, length)

    def products_of(head):
        cols = slice(head * HEAD_DIM, (head + 1) * HEAD_DIM)
        scores = nt(k_ext[keys, cols], q_ext[16 : 16 + tokens, cols])
        return jnp.where(inside, scores * FACTOR, LOW), nt(v_ext[keys, cols], d_attn[:, cols])

    heads = width // HEAD_DIM
    products = products_of(0)
    for head in range(heads):
        later = products_of(head + 1) if head + 1 < heads else None
        cols = slice(head * HEAD_DIM, (head + 1) * HEAD_DIM)
        scores, d_probs = products
        probs = jnp.exp(scores - by_row[4 + head : 5 + head, :])
        d_scores = (probs * (d_probs - by_row[head : head + 1, :])).astype(BF16)
        d_k[:, cols] = nn(d_scores[own], q_ext[16 : 16 + tokens, cols]) * FACTOR
        d_v[:, cols] = nn(probs[own].astype(BF16), d_attn[:, cols])
        d_q[:, cols] = (tn(k_ext[keys, cols], d_scores) * FACTOR).T.astype(BF16)
        products = later


def grouped(bits):
    pairs = [bits[at : at + 2] for at in range(0, len(bits), 2)]
    return [pair + [pair[0] ^ pair[1]] if len(pair) == 2 else pair for pair in pairs]


def packed(totals):
    rounded = lax.reduce_precision(totals[:TAPS], 8, 7)
    first = lax.reduce_precision(totals[TAPS:], 8, 7)
    second = lax.reduce_precision(totals[TAPS:] - first, 8, 7)
    third = totals[TAPS:] - first - second
    return jnp.concatenate([rounded, first, second, third], axis=0).astype(BF16)


def unpacked(sent):
    wide = sent.astype(F32)
    last = wide[TAPS : TAPS + 1] + wide[TAPS + 1 : TAPS + 2] + wide[TAPS + 2 : TAPS + 3]
    return jnp.concatenate([wide[:TAPS], last], axis=0)


def added(parts):
    sums = [unpacked(part) for part in parts]
    while len(sums) > 1:
        sums = [sums[at] + sums[at + 1] for at in range(0, len(sums), 2)]
    return sums[0]


def finish_kernel(info, k_part, v_part, near, far, *refs):
    parts, (d_k, d_v, d_conv, loss) = refs[:-4], refs[-4:]
    tokens, width = d_k.shape
    even = info[3] == 0
    for got, on_right in ((near, even), (far, ~even)):
        rows = pl.ds(pl.multiple_of(jnp.where(on_right, tokens - WINDOW, 0), WINDOW), WINDOW)
        for out, part, cols in (
            (d_k, k_part, slice(0, width)),
            (d_v, v_part, slice(width, 2 * width)),
        ):
            out[rows, :] = (part[rows, :] + got[:, cols].astype(F32)).astype(BF16)
    taps = [part[...].astype(F32)[0:TAPS] for part in parts]
    sums = []
    for part in parts:
        wide = part[...].astype(F32)
        sums.append(wide[TAPS : TAPS + 1] + wide[TAPS + 1 : TAPS + 2] + wide[TAPS + 2 : TAPS + 3])
    while len(taps) > 1:
        taps = [taps[at] + taps[at + 1] for at in range(0, len(taps), 2)]
        sums = [sums[at] + sums[at + 1] for at in range(0, len(sums), 2)]
    count = sums[0][:, 1:2]
    d_conv[...] = taps[0] / jnp.sqrt(count)
    loss[...] = sums[0][:, 0:1] / count


def call(kernel, operands, outs, scratch, places, flops, limit=24):
    specs = {
        "s": pl.BlockSpec(memory_space=pltpu.SMEM),
        "v": pl.BlockSpec(memory_space=pltpu.VMEM),
        "a": pl.BlockSpec(memory_space=pl.ANY),
    }
    arrays = list(operands) + list(outs)
    size = sum(math.prod(item.shape) * item.dtype.itemsize for item in arrays) if flops else 1
    return pl.pallas_call(
        kernel,
        out_shape=outs,
        in_specs=[specs[place] for place in places],
        out_specs=[specs["v"] for _ in outs],
        scratch_shapes=scratch,
        compiler_params=pltpu.CompilerParams(vmem_limit_bytes=limit * 1024 * 1024),
        cost_estimate=pl.CostEstimate(flops=max(flops, 1), bytes_accessed=size, transcendentals=0),
    )(*operands)


def local(
    queries,
    key_rows,
    value_rows,
    out_weight,
    head_weight,
    conv_weight,
    lengths,
    label_mask,
    targets,
):
    tokens, width = queries.shape[1:]
    depth = out_weight.shape[1]
    vocab = head_weight.shape[1]
    dp_size = lax.axis_size("dp")
    place = lax.axis_index("ctx")
    q, k, v = queries[0], key_rows[0], value_rows[0]
    info = jnp.stack([lengths[0], place * tokens, lax.axis_index("dp"), place % 2])
    info = info.astype(jnp.int32)

    shape = jax.ShapeDtypeStruct
    halo = shape((HALO, 2 * width), BF16)
    block = shape((tokens, width), BF16)
    near, far, meta = call(
        pack_kernel,
        (targets, label_mask, q, k, v),
        (halo, halo, shape((tokens, 128), F32)),
        [
            pltpu.VMEM((2, 2 * EDGE, width), BF16),
            pltpu.VMEM((2, 1, tokens), jnp.int32),
            pltpu.SemaphoreType.DMA((8,)),
        ],
        "aaaaa",
        0,
        56,
    )
    q_own, k_own, v_own = call(stage_kernel, (q, k, v), (block, block, block), [], "vvv", 0)
    near, far, head_weight = lax.optimization_barrier((near, far, head_weight))
    near, far = exchanged(near, far, "ctx")
    top_bit = bits_of(dp_size)[-1]
    far_out = swapped(out_weight, "dp", top_bit)
    far_head = swapped(head_weight, "dp", top_bit)
    out_marks, out_held = spread([(0, out_weight), (top_bit, far_out)], "dp")
    near, far, *out_held = lax.optimization_barrier((near, far, *out_held))

    ext = tokens + 2 * EDGE
    attn, lse, k_ext, v_ext, q_ext, meta_edges = call(
        attention_kernel,
        (info, q_own, k_own, v_own, near, far),
        (
            shape((tokens + 32, width), BF16),
            shape((tokens, 128), F32),
            shape((tokens + 2 * HALO, width), BF16),
            shape((tokens + 2 * HALO, width), BF16),
            shape((tokens + 32, width), BF16),
            shape((2 * EDGE, 128), F32),
        ),
        [],
        "svvvvv",
        4 * tokens * 3 * WINDOW * width,
    )
    attn, far_head = lax.optimization_barrier((attn, far_head))
    own_marks, own_held = spread([(0, head_weight)], "dp")
    far_marks, far_held = spread([(top_bit, far_head)], "dp")
    head_marks, head_held = own_marks + far_marks, own_held + far_held

    chunks = depth // 128
    hid, out_full, gated, slope = call(
        functools.partial(hidden_kernel, out_marks),
        (info, attn, conv_weight, *out_held),
        (
            shape((chunks, ext + 2 * EDGE, 128), F32),
            shape((width, depth), BF16),
            shape((ext, depth), BF16),
            shape((chunks, ext, 128), F32),
        ),
        [pltpu.SemaphoreType.DMA((len(out_held),))],
        "svv" + "a" * len(out_held),
        2 * tokens * depth * width,
    )
    d_attn, stats, summary = call(
        functools.partial(middle_kernel, head_marks),
        (info, attn, lse, meta, meta_edges, conv_weight, hid, out_full, gated, slope, *head_held),
        (
            shape((tokens, width), BF16),
            shape((tokens, 128), F32),
            shape((16, depth), F32),
        ),
        [
            pltpu.VMEM((depth // 2, vocab), BF16),
            pltpu.VMEM((depth // 2, vocab), BF16),
            pltpu.VMEM((ext, vocab), F32),
            pltpu.VMEM((ext, vocab), BF16),
            pltpu.VMEM((chunks, ext, 128), F32),
            pltpu.VMEM((tokens, depth), BF16),
            pltpu.SemaphoreType.DMA((len(head_held),)),
        ],
        "svvvvvvvvv" + "a" * len(head_held),
        4 * tokens * depth * (width + vocab),
    )

    totals = summary[: TAPS + 1]
    dp_bits, ctx_bits = bits_of(dp_size), bits_of(lax.axis_size("ctx"))
    near_part, far_part = call(
        edge_grads_kernel,
        (info, q_ext, k_ext, v_ext, stats, d_attn),
        (shape((WINDOW, 2 * width), BF16), shape((WINDOW, 2 * width), BF16)),
        [],
        "svvvvv",
        16 * WINDOW * WINDOW * width,
    )
    steps = [("ctx", ctx_bits[:1])]
    steps += [("dp", group) for group in grouped(dp_bits)]
    steps += [("ctx", group) for group in grouped(ctx_bits[1:])]
    for index, (axis, group) in enumerate(steps):
        sent = packed(totals)
        got = [swapped(sent, axis, bit) for bit in group]
        if index == 0:
            near_part, far_part, d_attn, *got = lax.optimization_barrier(
                (near_part, far_part, d_attn, *got)
            )
            near_got, far_got = exchanged(near_part, far_part, "ctx")
        if index == len(steps) - 1:
            d_q, k_part, v_part = call(
                own_grads_kernel,
                (info, q_ext, k_ext, v_ext, stats, d_attn),
                (block, shape((tokens, width), F32), shape((tokens, width), F32)),
                [],
                "svvvvv",
                0,
            )
            d_q, k_part, v_part, *got = lax.optimization_barrier((d_q, k_part, v_part, *got))
        if index < len(steps) - 1:
            totals = added([sent] + got)
    d_k, d_v, d_conv, loss = call(
        finish_kernel,
        (info, k_part, v_part, near_got, far_got, sent, *got),
        (block, block, shape((TAPS, depth), F32), shape((1, 1), F32)),
        [],
        "svvvv" + "v" * (1 + len(got)),
        tokens * width,
    )
    return (loss[0, 0], d_q[None], d_k[None], d_v[None], d_conv)


def solution(mesh):
    placed = (
        P("dp", "ctx", None),
        P("dp", "ctx", None),
        P("dp", "ctx", None),
        P("dp", None),
        P("dp", None),
        P(),
        P("dp"),
        P("dp", "ctx"),
        P("dp", "ctx"),
    )
    return jax.shard_map(
        local,
        mesh=mesh,
        in_specs=placed,
        out_specs=(P(), P("dp", "ctx", None), P("dp", "ctx", None), P("dp", "ctx", None), P()),
        check_vma=False,
    )
```

```python
import functools
import math

import jax
import jax.numpy as jnp
from jax import lax
from jax.experimental import pallas as pl
from jax.experimental.pallas import tpu as pltpu
from jax.sharding import PartitionSpec as P

HEAD_DIM = 128
WINDOW = 128
TAPS = 9
MARGIN = (TAPS - 1) // 2
EDGE = 8
HALO = WINDOW + 2 * EDGE
LOW = -1e30
FACTOR = 1.0 / math.sqrt(HEAD_DIM)
F32 = jnp.float32
BF16 = jnp.bfloat16


def bits_of(size):
    bits = []
    while (1 << len(bits)) < size:
        bits.append(1 << len(bits))
    return bits


def swapped(value, axis, bit):
    size = lax.axis_size(axis)
    return lax.ppermute(value, axis, [(i, i ^ bit) for i in range(size)])


def spread(pieces, axis):
    for bit in reversed(bits_of(lax.axis_size(axis))[:-1]):
        pieces = pieces + [(mark ^ bit, swapped(item, axis, bit)) for mark, item in pieces]
    return [mark for mark, _ in pieces], [item for _, item in pieces]


def exchanged(near, far, axis):
    size = lax.axis_size(axis)
    pairs = [(i, i ^ 1) for i in range(size) if (i ^ 1) < size]
    others = [(i, i - 1 + 2 * (i % 2)) for i in range(size) if 0 <= i - 1 + 2 * (i % 2) < size]
    return lax.ppermute(near, axis, pairs), lax.ppermute(far, axis, others)


def nt(left, right):
    return lax.dot_general(left, right, (((1,), (1,)), ((), ())), preferred_element_type=F32)


def tn(left, right):
    return lax.dot_general(left, right, (((0,), (0,)), ((), ())), preferred_element_type=F32)


def nn(left, right):
    return jnp.dot(left, right, preferred_element_type=F32)


def in_reach(query_pos, key_pos, offset, length):
    return (
        (jnp.abs(query_pos - key_pos) <= WINDOW)
        & (key_pos + offset >= 0)
        & (key_pos + offset < length)
    )


def pack_kernel(targets, mask, q, k, v, near, far, meta, edges, marks, sems):
    tokens, width = q.shape
    even = lax.rem(lax.axis_index("ctx"), 2) == 0
    edge = 2 * EDGE
    ends = (slice(0, edge), slice(tokens - edge, tokens))
    copies = []

    def fetch(source, target):
        copy = pltpu.make_async_copy(source, target, sems.at[len(copies)])
        copy.start()
        copies.append(copy)

    start = pl.multiple_of(jnp.where(even, tokens - HALO, 0), 16)
    other = pl.multiple_of(jnp.where(even, 0, tokens - HALO), 16)
    for message, first in ((near, start), (far, other)):
        fetch(k.at[pl.ds(first, HALO)], message.at[:, 0:width])
        fetch(v.at[pl.ds(first, HALO)], message.at[:, width : 2 * width])
    for place, end in enumerate(ends):
        fetch(q.at[end], edges.at[place])
    fetch(targets, marks.at[0])
    fetch(mask, marks.at[1])
    for copy in copies[-2:]:
        copy.wait()
    spread = (128, tokens)
    target = jnp.broadcast_to(marks[0], spread).T
    chosen = jnp.broadcast_to(marks[1], spread).T
    spot = lax.broadcasted_iota(jnp.int32, (tokens, 128), 1)
    entry = jnp.where(spot == 0, target >> 5, jnp.where(spot == 1, target & 31, chosen))
    meta[...] = entry.astype(F32)
    for copy in copies[:-2]:
        copy.wait()
    low = lax.broadcasted_iota(jnp.int32, (edge, 1), 0) < EDGE

    def patch(message, place, use, end):
        rows = slice(place, place + edge)
        held = message[rows, :].astype(F32)
        ours = jnp.concatenate(
            [edges[end].astype(F32), meta[ends[end], :], jnp.zeros((edge, width - 128), F32)],
            axis=1,
        )
        ours = jnp.concatenate([ours[EDGE:], ours[:EDGE]], axis=0)
        message[rows, :] = jnp.where(use, ours, held).astype(BF16)

    @pl.when(even)
    def _():
        patch(near, 0, low, 1)
        patch(far, HALO - edge, ~low, 0)

    @pl.when(~even)
    def _():
        patch(near, HALO - edge, ~low, 0)
        patch(far, 0, low, 1)


def stage_kernel(q, k, v, q_own, k_own, v_own):
    q_own[...] = q[...]
    k_own[...] = k[...]
    v_own[...] = v[...]


def attention_kernel(
    info, q, k, v, near, far, attn, lse, k_ext, v_ext, q_ext, meta_edges
):
    tokens, width = q.shape
    length, offset = info[0], info[1]
    even = info[3] == 0
    q_ext[16 : 16 + tokens, :] = q[...]
    k_ext[HALO : HALO + tokens, :] = k[...]
    v_ext[HALO : HALO + tokens, :] = v[...]

    def place_sides(left, right):
        for ext, first in ((k_ext, 0), (v_ext, width)):
            cols = slice(first, first + width)
            ext[0:HALO, :] = left[:, cols]
            ext[HALO + tokens : 2 * HALO + tokens, :] = right[:, cols]
        q_ext[0:16, :] = left[0:16, 0:width]
        q_ext[16 + tokens :, :] = right[HALO - 16 : HALO, 0:width]
        spots = slice(width, width + 128)
        meta_edges[0:EDGE, :] = left[0:16, spots].astype(F32)[0:EDGE]
        meta_edges[EDGE:, :] = right[HALO - 16 : HALO, spots].astype(F32)[EDGE:]

    @pl.when(even)
    def _():
        place_sides(far, near)

    @pl.when(~even)
    def _():
        place_sides(near, far)

    lse[...] = jnp.zeros(lse.shape, F32)
    rows, span = 16 + WINDOW, 4 * WINDOW
    spot = lax.broadcasted_iota(jnp.int32, (rows, span), 0)
    blocks = [
        (0, 0, jnp.where(spot < EDGE, spot - EDGE, spot - 16)),
        (
            tokens + 32 - rows,
            tokens + 2 * HALO - span,
            jnp.where(spot < WINDOW, spot + tokens - WINDOW, spot + tokens - WINDOW - EDGE),
        ),
    ]
    work = []
    for place, key_row, query_pos in blocks:
        key_pos = key_row - HALO + lax.broadcasted_iota(jnp.int32, (rows, span), 1)
        inside = in_reach(query_pos, key_pos, offset, length)
        keys = slice(key_row, key_row + span)
        work += [(place, keys, inside, at) for at in range(0, width, HEAD_DIM)]

    def scores_of(item):
        place, keys, inside, at = item
        cols = slice(at, at + HEAD_DIM)
        product = nt(q_ext[place : place + rows, cols], k_ext[keys, cols])
        return jnp.where(inside, product * FACTOR, LOW)

    scores = scores_of(work[0])
    for index, (place, keys, _, at) in enumerate(work):
        later = scores_of(work[index + 1]) if index + 1 < len(work) else None
        cols = slice(at, at + HEAD_DIM)
        head = at // HEAD_DIM
        top = jnp.max(scores, axis=-1, keepdims=True)
        grown = jnp.exp(scores - top)
        total = jnp.sum(grown, axis=-1, keepdims=True)
        mixed = nn(grown.astype(BF16), v_ext[keys, cols]) * (1.0 / total)
        attn[place : place + rows, cols] = mixed.astype(BF16)
        level = top + jnp.log(total)
        first = max(place, 16)
        lse[first - 16 : first - 16 + WINDOW, 4 + head : 5 + head] = level[
            first - place : first - place + WINDOW
        ]
        scores = later


def fetch_pieces(marks, mine, pieces, full, sems, first=0):
    copies = []
    held = full.shape[0] // pieces[0].shape[0]
    for mark, piece in zip(marks, pieces):
        rows = piece.shape[0]
        start = ((mine ^ mark) & (held - 1)) * rows
        target = full.at[pl.ds(pl.multiple_of(start, rows), rows)]
        copies.append(pltpu.make_async_copy(piece, target, sems.at[first + len(copies)]))
        copies[-1].start()
    return copies


def live_rows(info, rows, lanes):
    row_pos = info[1] - EDGE + lax.broadcasted_iota(jnp.int32, (rows, lanes), 0)
    return (row_pos >= 0) & (row_pos < info[0])


def hidden_kernel(marks, info, attn, taps, *refs):
    pieces, (hid, out_full, gated, slope, sems) = refs[: len(marks)], refs[len(marks) :]
    copies = fetch_pieces(marks, info[2], pieces, out_full, sems)
    chunks, ext, lanes = hid.shape
    depth = chunks * lanes
    ext = ext - 2 * EDGE
    live = live_rows(info, ext, lanes)
    hid[:, 0:EDGE, :] = jnp.zeros((chunks, EDGE, lanes), F32)
    hid[:, EDGE + ext :, :] = jnp.zeros((chunks, EDGE, lanes), F32)
    for copy in copies:
        copy.wait()
    last = attn.shape[0] - 16
    for at in range(0, chunks * lanes, 256):
        block = nn(attn[...], out_full[:, at : at + 256])
        block = jnp.concatenate([block[0:EDGE], block[16:last], block[last + EDGE :]], axis=0)
        for part in range(2):
            piece = block[:, part * lanes : (part + 1) * lanes]
            hid[at // lanes + part, EDGE : EDGE + ext, :] = jnp.where(live, piece, 0.0)
    for chunk in range(depth // lanes):
        cols = slice(chunk * lanes, (chunk + 1) * lanes)
        conv = jnp.zeros((ext, lanes), F32)
        for tap in range(TAPS):
            start = EDGE - MARGIN + tap
            conv = conv + taps[tap : tap + 1, cols] * hid[chunk, start : start + ext, :]
        sigma = jax.nn.sigmoid(conv)
        gated[:, cols] = (conv * sigma).astype(BF16)
        slope[chunk] = sigma * (1.0 + conv * (1.0 - sigma))


def middle_kernel(
    marks, info, attn, lse, meta, meta_edges, taps, hid, out_full, gated, slope, *refs
):
    pieces, (d_attn, stats, summary) = refs[: len(marks)], refs[len(marks) : len(marks) + 3]
    head_own, head_far, logits, d_logits, d_pre, d_hid, sems = refs[len(marks) + 3 :]
    count = len(marks) // 2
    others = fetch_pieces(marks[:count], info[2], pieces[:count], head_own, sems)
    copies = fetch_pieces(marks[count:], info[2], pieces[count:], head_far, sems, count)
    tokens, width = d_attn.shape
    half, vocab = head_far.shape
    depth = 2 * half
    on_top = (info[2] & count) != 0
    own_start = pl.multiple_of(jnp.where(on_top, half, 0), half)
    far_start = pl.multiple_of(jnp.where(on_top, 0, half), half)
    ext = tokens + 2 * EDGE
    lanes = 128
    live = live_rows(info, ext, lanes)
    for copy in others:
        copy.wait()
    for at in range(0, vocab, 256):
        cols = slice(at, at + 256)
        logits[:, cols] = nn(gated[:, pl.ds(own_start, half)], head_own[:, cols])
    for copy in copies:
        copy.wait()
    for at in range(0, vocab, 256):
        cols = slice(at, at + 256)
        logits[:, cols] += nn(gated[:, pl.ds(far_start, half)], head_far[:, cols])
    meta_all = jnp.concatenate([meta_edges[0:EDGE], meta[...], meta_edges[EDGE:]], axis=0)
    target = (meta_all[:, 0:1] * 32.0 + meta_all[:, 1:2]).astype(jnp.int32)
    chosen = jnp.where(live & (meta_all[:, 2:3] == 1.0), 1.0, 0.0)[:, 0:1]
    loss_rows = jnp.zeros((16, 1), F32)
    count_rows = jnp.zeros((16, 1), F32)
    word = lax.broadcasted_iota(jnp.int32, (16, vocab), 1)
    row_in = lax.broadcasted_iota(jnp.int32, (16, 1), 0)
    for at in range(0, ext, 16):
        block = logits[at : at + 16, :]
        top = jnp.max(block, axis=-1, keepdims=True)
        grown = jnp.exp(block - top)
        total = jnp.sum(grown, axis=-1, keepdims=True)
        hit = target[at : at + 16] == word
        picked = jnp.sum(jnp.where(hit, block, 0.0), axis=-1, keepdims=True)
        pick = chosen[at : at + 16]
        change = grown * (pick / total) - jnp.where(hit, pick, 0.0)
        d_logits[at : at + 16, :] = change.astype(BF16)
        own = (row_in + at >= EDGE) & (row_in + at < EDGE + tokens)
        kept = jnp.where(own, pick, 0.0)
        loss_rows = loss_rows + kept * (top + jnp.log(total) - picked)
        count_rows = count_rows + kept
    summary[...] = jnp.zeros(summary.shape, F32)
    lane = lax.broadcasted_iota(jnp.int32, (1, lanes), 1)
    loss_sum = jnp.sum(loss_rows, axis=0, keepdims=True)
    count_sum = jnp.sum(count_rows, axis=0, keepdims=True)
    summary[TAPS : TAPS + 1, 0:lanes] = jnp.where(
        lane == 0, loss_sum, jnp.where(lane == 1, count_sum, 0.0)
    )
    turns = [
        (held, start, at)
        for held, start in ((head_own, own_start), (head_far, far_start))
        for at in range(0, half, 256)
    ]
    d_gated = nt(d_logits[...], head_own[0:256, :])
    for turn, (_, start, at) in enumerate(turns):
        later = None
        if turn + 1 < len(turns):
            held, _, following = turns[turn + 1]
            later = nt(d_logits[...], held[following : following + 256, :])
        for part in range(2):
            chunk = start // lanes + at // lanes + part
            cols = pl.ds(pl.multiple_of(start + at + part * lanes, lanes), lanes)
            change = d_gated[:, part * lanes : (part + 1) * lanes] * slope[chunk]
            d_pre[chunk] = change
            owned = change[EDGE : EDGE + tokens]
            for tap in range(TAPS):
                row = 2 * EDGE - MARGIN + tap
                summary[tap : tap + 1, cols] = jnp.sum(
                    owned * hid[chunk, row : row + tokens, :], axis=0, keepdims=True
                )
        d_gated = later
    for chunk in range(depth // lanes):
        cols = slice(chunk * lanes, (chunk + 1) * lanes)
        change = jnp.zeros((tokens, lanes), F32)
        for tap in range(TAPS):
            start = EDGE + MARGIN - tap
            change = change + taps[tap : tap + 1, cols] * d_pre[chunk, start : start + tokens, :]
        d_hid[:, cols] = jnp.where(live[EDGE : EDGE + tokens], change, 0.0).astype(BF16)
    stats[...] = lse[...]
    blocks = [
        nt(d_hid[...], out_full[at : at + 2 * HEAD_DIM, :]).astype(BF16)
        for at in range(0, width, 2 * HEAD_DIM)
    ]
    for place, pair in enumerate(blocks):
        for part in range(2):
            head = 2 * place + part
            cols = slice(head * HEAD_DIM, (head + 1) * HEAD_DIM)
            block = pair[:, part * HEAD_DIM : (part + 1) * HEAD_DIM]
            d_attn[:, cols] = block
            products = block.astype(F32) * attn[16 : 16 + tokens, cols].astype(F32)
            stats[:, head : head + 1] = jnp.sum(products, axis=-1, keepdims=True)


def edge_grads_kernel(info, q_ext, k_ext, v_ext, stats, d_attn, near, far):
    tokens, width = d_attn.shape
    length, offset = info[0], info[1]
    even = info[3] == 0
    work = []
    for out, on_right in ((near, even), (far, ~even)):
        first = pl.multiple_of(jnp.where(on_right, tokens - WINDOW, 0), WINDOW)
        key_start = jnp.where(on_right, tokens, -WINDOW)
        rows = pl.ds(first, WINDOW)
        asked = pl.ds(pl.multiple_of(first + 16, 16), WINDOW)
        keys = pl.ds(pl.multiple_of(key_start + HALO, 16), WINDOW)
        by_row = stats[rows, :].T
        key_pos = key_start + lax.broadcasted_iota(jnp.int32, (WINDOW, WINDOW), 0)
        query_pos = first + lax.broadcasted_iota(jnp.int32, (WINDOW, WINDOW), 1)
        inside = in_reach(query_pos, key_pos, offset, length)
        for head in range(width // HEAD_DIM):
            cols = slice(head * HEAD_DIM, (head + 1) * HEAD_DIM)
            query, change = q_ext[asked, cols], d_attn[rows, cols]
            scores = jnp.where(inside, nt(k_ext[keys, cols], query) * FACTOR, LOW)
            d_probs = nt(v_ext[keys, cols], change)
            work.append((out, head, by_row, query, change, scores, d_probs))
    done = []
    for out, head, by_row, query, change, scores, d_probs in work:
        probs = jnp.exp(scores - by_row[4 + head : 5 + head, :])
        d_scores = probs * (d_probs - by_row[head : head + 1, :])
        done.append((out, head, query, change, d_scores.astype(BF16), probs.astype(BF16)))
    for out, head, query, change, d_scores, probs in done:
        cols = slice(head * HEAD_DIM, (head + 1) * HEAD_DIM)
        out[:, cols] = (nn(d_scores, query) * FACTOR).astype(BF16)
        cols = slice(width + head * HEAD_DIM, width + (head + 1) * HEAD_DIM)
        out[:, cols] = nn(probs, change).astype(BF16)


def own_grads_kernel(info, q_ext, k_ext, v_ext, stats, d_attn, d_q, d_k, d_v):
    tokens, width = d_attn.shape
    length, offset = info[0], info[1]
    span = tokens + 2 * WINDOW
    keys = slice(HALO - WINDOW, HALO + tokens + WINDOW)
    own = slice(WINDOW, WINDOW + tokens)
    by_row = stats[...].T
    key_pos = lax.broadcasted_iota(jnp.int32, (span, tokens), 0) - WINDOW
    query_pos = lax.broadcasted_iota(jnp.int32, (span, tokens), 1)
    inside = in_reach(query_pos, key_pos, offset, length)

    def products_of(head):
        cols = slice(head * HEAD_DIM, (head + 1) * HEAD_DIM)
        scores = nt(k_ext[keys, cols], q_ext[16 : 16 + tokens, cols])
        return jnp.where(inside, scores * FACTOR, LOW), nt(v_ext[keys, cols], d_attn[:, cols])

    heads = width // HEAD_DIM
    products = products_of(0)
    for head in range(heads):
        later = products_of(head + 1) if head + 1 < heads else None
        cols = slice(head * HEAD_DIM, (head + 1) * HEAD_DIM)
        scores, d_probs = products
        probs = jnp.exp(scores - by_row[4 + head : 5 + head, :])
        d_scores = (probs * (d_probs - by_row[head : head + 1, :])).astype(BF16)
        d_k[:, cols] = nn(d_scores[own], q_ext[16 : 16 + tokens, cols]) * FACTOR
        d_v[:, cols] = nn(probs[own].astype(BF16), d_attn[:, cols])
        d_q[:, cols] = (tn(k_ext[keys, cols], d_scores) * FACTOR).T.astype(BF16)
        products = later


def grouped(bits):
    pairs = [bits[at : at + 2] for at in range(0, len(bits), 2)]
    return [pair + [pair[0] ^ pair[1]] if len(pair) == 2 else pair for pair in pairs]


def packed(totals):
    rounded = lax.reduce_precision(totals[:TAPS], 8, 7)
    first = lax.reduce_precision(totals[TAPS:], 8, 7)
    second = lax.reduce_precision(totals[TAPS:] - first, 8, 7)
    third = totals[TAPS:] - first - second
    return jnp.concatenate([rounded, first, second, third], axis=0).astype(BF16)


def unpacked(sent):
    wide = sent.astype(F32)
    last = wide[TAPS : TAPS + 1] + wide[TAPS + 1 : TAPS + 2] + wide[TAPS + 2 : TAPS + 3]
    return jnp.concatenate([wide[:TAPS], last], axis=0)


def added(parts):
    sums = [unpacked(part) for part in parts]
    while len(sums) > 1:
        sums = [sums[at] + sums[at + 1] for at in range(0, len(sums), 2)]
    return sums[0]


def finish_kernel(info, k_part, v_part, near, far, *refs):
    parts, (d_k, d_v, d_conv, loss) = refs[:-4], refs[-4:]
    tokens, width = d_k.shape
    even = info[3] == 0
    for got, on_right in ((near, even), (far, ~even)):
        rows = pl.ds(pl.multiple_of(jnp.where(on_right, tokens - WINDOW, 0), WINDOW), WINDOW)
        for out, part, cols in (
            (d_k, k_part, slice(0, width)),
            (d_v, v_part, slice(width, 2 * width)),
        ):
            out[rows, :] = (part[rows, :] + got[:, cols].astype(F32)).astype(BF16)
    taps = [part[...].astype(F32)[0:TAPS] for part in parts]
    sums = []
    for part in parts:
        wide = part[...].astype(F32)
        sums.append(wide[TAPS : TAPS + 1] + wide[TAPS + 1 : TAPS + 2] + wide[TAPS + 2 : TAPS + 3])
    while len(taps) > 1:
        taps = [taps[at] + taps[at + 1] for at in range(0, len(taps), 2)]
        sums = [sums[at] + sums[at + 1] for at in range(0, len(sums), 2)]
    count = sums[0][:, 1:2]
    d_conv[...] = taps[0] / jnp.sqrt(count)
    loss[...] = sums[0][:, 0:1] / count


def call(kernel, operands, outs, scratch, places, flops, limit=24):
    specs = {
        "s": pl.BlockSpec(memory_space=pltpu.SMEM),
        "v": pl.BlockSpec(memory_space=pltpu.VMEM),
        "a": pl.BlockSpec(memory_space=pl.ANY),
    }
    arrays = list(operands) + list(outs)
    size = sum(math.prod(item.shape) * item.dtype.itemsize for item in arrays) if flops else 1
    return pl.pallas_call(
        kernel,
        out_shape=outs,
        in_specs=[specs[place] for place in places],
        out_specs=[specs["v"] for _ in outs],
        scratch_shapes=scratch,
        compiler_params=pltpu.CompilerParams(vmem_limit_bytes=limit * 1024 * 1024),
        cost_estimate=pl.CostEstimate(flops=max(flops, 1), bytes_accessed=size, transcendentals=0),
    )(*operands)


def local(
    queries,
    key_rows,
    value_rows,
    out_weight,
    head_weight,
    conv_weight,
    lengths,
    label_mask,
    targets,
):
    tokens, width = queries.shape[1:]
    depth = out_weight.shape[1]
    vocab = head_weight.shape[1]
    dp_size = lax.axis_size("dp")
    place = lax.axis_index("ctx")
    q, k, v = queries[0], key_rows[0], value_rows[0]
    info = jnp.stack([lengths[0], place * tokens, lax.axis_index("dp"), place % 2])
    info = info.astype(jnp.int32)

    shape = jax.ShapeDtypeStruct
    halo = shape((HALO, 2 * width), BF16)
    block = shape((tokens, width), BF16)
    near, far, meta = call(
        pack_kernel,
        (targets, label_mask, q, k, v),
        (halo, halo, shape((tokens, 128), F32)),
        [
            pltpu.VMEM((2, 2 * EDGE, width), BF16),
            pltpu.VMEM((2, 1, tokens), jnp.int32),
            pltpu.SemaphoreType.DMA((8,)),
        ],
        "aaaaa",
        0,
        56,
    )
    q_own, k_own, v_own = call(stage_kernel, (q, k, v), (block, block, block), [], "vvv", 0)
    near, far, head_weight = lax.optimization_barrier((near, far, head_weight))
    near, far = exchanged(near, far, "ctx")
    top_bit = bits_of(dp_size)[-1]
    far_out = swapped(out_weight, "dp", top_bit)
    far_head = swapped(head_weight, "dp", top_bit)
    out_marks, out_held = spread([(0, out_weight), (top_bit, far_out)], "dp")
    near, far, *out_held = lax.optimization_barrier((near, far, *out_held))

    ext = tokens + 2 * EDGE
    attn, lse, k_ext, v_ext, q_ext, meta_edges = call(
        attention_kernel,
        (info, q_own, k_own, v_own, near, far),
        (
            shape((tokens + 32, width), BF16),
            shape((tokens, 128), F32),
            shape((tokens + 2 * HALO, width), BF16),
            shape((tokens + 2 * HALO, width), BF16),
            shape((tokens + 32, width), BF16),
            shape((2 * EDGE, 128), F32),
        ),
        [],
        "svvvvv",
        4 * tokens * 3 * WINDOW * width,
    )
    attn, far_head = lax.optimization_barrier((attn, far_head))
    own_marks, own_held = spread([(0, head_weight)], "dp")
    far_marks, far_held = spread([(top_bit, far_head)], "dp")
    head_marks, head_held = own_marks + far_marks, own_held + far_held

    chunks = depth // 128
    hid, out_full, gated, slope = call(
        functools.partial(hidden_kernel, out_marks),
        (info, attn, conv_weight, *out_held),
        (
            shape((chunks, ext + 2 * EDGE, 128), F32),
            shape((width, depth), BF16),
            shape((ext, depth), BF16),
            shape((chunks, ext, 128), F32),
        ),
        [pltpu.SemaphoreType.DMA((len(out_held),))],
        "svv" + "a" * len(out_held),
        2 * tokens * depth * width,
    )
    d_attn, stats, summary = call(
        functools.partial(middle_kernel, head_marks),
        (info, attn, lse, meta, meta_edges, conv_weight, hid, out_full, gated, slope, *head_held),
        (
            shape((tokens, width), BF16),
            shape((tokens, 128), F32),
            shape((16, depth), F32),
        ),
        [
            pltpu.VMEM((depth // 2, vocab), BF16),
            pltpu.VMEM((depth // 2, vocab), BF16),
            pltpu.VMEM((ext, vocab), F32),
            pltpu.VMEM((ext, vocab), BF16),
            pltpu.VMEM((chunks, ext, 128), F32),
            pltpu.VMEM((tokens, depth), BF16),
            pltpu.SemaphoreType.DMA((len(head_held),)),
        ],
        "svvvvvvvvv" + "a" * len(head_held),
        4 * tokens * depth * (width + vocab),
    )

    totals = summary[: TAPS + 1]
    dp_bits, ctx_bits = bits_of(dp_size), bits_of(lax.axis_size("ctx"))
    near_part, far_part = call(
        edge_grads_kernel,
        (info, q_ext, k_ext, v_ext, stats, d_attn),
        (shape((WINDOW, 2 * width), BF16), shape((WINDOW, 2 * width), BF16)),
        [],
        "svvvvv",
        16 * WINDOW * WINDOW * width,
    )
    steps = [("ctx", ctx_bits[:1])]
    steps += [("dp", group) for group in grouped(dp_bits)]
    steps += [("ctx", group) for group in grouped(ctx_bits[1:])]
    for index, (axis, group) in enumerate(steps):
        sent = packed(totals)
        got = [swapped(sent, axis, bit) for bit in group]
        if index == 0:
            near_got, far_got = exchanged(near_part, far_part, "ctx")
            _, _, d_attn, *got = lax.optimization_barrier((near_part, far_part, d_attn, *got))
        if index == 1:
            d_q, k_part, v_part = call(
                own_grads_kernel,
                (info, q_ext, k_ext, v_ext, stats, d_attn),
                (block, shape((tokens, width), F32), shape((tokens, width), F32)),
                [],
                "svvvvv",
                0,
            )
            d_q, k_part, v_part, *got = lax.optimization_barrier((d_q, k_part, v_part, *got))
        if index < len(steps) - 1:
            totals = added([sent] + got)
    d_k, d_v, d_conv, loss = call(
        finish_kernel,
        (info, k_part, v_part, near_got, far_got, sent, *got),
        (block, block, shape((TAPS, depth), F32), shape((1, 1), F32)),
        [],
        "svvvv" + "v" * (1 + len(got)),
        tokens * width,
    )
    return (loss[0, 0], d_q[None], d_k[None], d_v[None], d_conv)


def solution(mesh):
    placed = (
        P("dp", "ctx", None),
        P("dp", "ctx", None),
        P("dp", "ctx", None),
        P("dp", None),
        P("dp", None),
        P(),
        P("dp"),
        P("dp", "ctx"),
        P("dp", "ctx"),
    )
    return jax.shard_map(
        local,
        mesh=mesh,
        in_specs=placed,
        out_specs=(P(), P("dp", "ctx", None), P("dp", "ctx", None), P("dp", "ctx", None), P()),
        check_vma=False,
    )
```
